256 devices in a mesh: cell: 16 (over x, y), gene: 16 (over z, core).
Axes of the slice: x: 4, y: 4, z: 8, core: 2. Of those that a mesh axis runs over, the one named last changes fastest.
Arguments:
- expression: bfloat16 [4096, 20480], P('cell', 'gene'), may hold values from -12 to 12
- mixing: bfloat16 [4, 256, 512], replicated, may hold values from -0.25 to 0.25
Outputs:
- basis: float32 [256, 20480], P(None, 'gene')
- scores: float32 [4096, 256], P('cell', 'gene')
The draws below stay inside these ranges and needn't reach their ends.
All inputs are finite; a program needn't handle non-finite values.
Results may differ from the reference program's by a relative error of at most 0.0006.
Values sent between devices are 32-bit elements; how exact they have to be, the bound alone decides.
A program may use at most 64 MiB of HBM per device.

```python
import jax
import jax.numpy as jnp
from jax import lax

GENES = 20480
ELL = 256
CELLS_DEV = 256
NS_ITERS = 8
FOLDS = 0
LEVELS = 4
SECTIONS = 4
CELLS = 4096
N_CELL = 16


def draw_expression(key, part):
    key = jax.random.fold_in(key, 7)
    keys = jax.random.split(key, 4)
    depth = jnp.exp(jax.random.uniform(keys[0], (CELLS, 1), jnp.float32, 0.0, 2.302585))
    spread = jnp.exp(jax.random.uniform(keys[1], (1, GENES), jnp.float32, 0.0, 2.302585))
    keep = jax.random.bernoulli(keys[2], 0.7, (CELLS, GENES)).astype(jnp.float32)
    base = jax.random.normal(keys[3], (CELLS, GENES), jnp.float32)
    values = 0.3 * jnp.sqrt(depth) * jnp.sqrt(spread) * base * keep
    return jnp.clip(values, -12.0, 12.0).astype(jnp.bfloat16)


def scatter_about(key, extent, width, most, kind=jnp.bfloat16):
    drawn = width * jax.random.normal(key, extent, jnp.float32)
    return jnp.clip(drawn, min=-most, max=most).astype(kind)


def setup_inputs(seed: int = 0) -> dict:
    key_of = jax.random.split(jax.random.key(seed), 3)
    return {
        "expression": draw_expression(jax.random.fold_in(key_of[2], 71), 0),
        "mixing": scatter_about(key_of[1], (SECTIONS, ELL, 2 * ELL), (2 * ELL) ** -0.5, 0.25),
    }


HIGH = lax.Precision.HIGHEST

def inner(left, right):
    return lax.dot_general(left, right, (((1,), (1,)), ((), ())), precision=HIGH, preferred_element_type=jnp.float32)

def product(left, right):
    return jnp.dot(left, right, precision=HIGH, preferred_element_type=jnp.float32)

def compressor(gram_full, mix):
    total = jnp.sqrt(jnp.sum(gram_full * gram_full) + 1e-06)
    eye = jnp.eye(gram_full.shape[0], dtype=jnp.float32)
    resid = eye - gram_full / total
    filt = eye - 0.5 * product(resid, resid)
    return product(mix.astype(jnp.float32), filt)

def shrink(stacked, mix):
    weights = compressor(inner(stacked, stacked), mix)
    return product(weights, stacked)

def reference(expression, mixing):
    batches = expression.reshape(N_CELL, CELLS_DEV, GENES)

    def fold_batch(batch):
        sketch = batch[:ELL].astype(jnp.float32)
        for k in range(FOLDS):
            fresh = batch[(k + 1) * ELL:(k + 2) * ELL].astype(jnp.float32)
            sketch = shrink(jnp.concatenate([sketch, fresh], axis=0), mixing[k])
        return sketch
    sketches = lax.map(fold_batch, batches)
    for level in range(LEVELS):
        pairs = sketches.reshape(-1, 2 * ELL, GENES)
        mix = mixing[FOLDS + level]
        sketches = lax.map(lambda stacked: shrink(stacked, mix), pairs)
    final = sketches[0]
    gram_full = inner(final, final)
    total = jnp.sqrt(jnp.sum(gram_full * gram_full) + 1e-06)
    eye = jnp.eye(ELL, dtype=jnp.float32)
    ymat = gram_full / total
    zmat = eye
    for step in range(NS_ITERS):
        middle = 0.5 * (3.0 * eye - product(zmat, ymat))
        ymat = product(ymat, middle)
        zmat = product(middle, zmat)
    basis = jnp.sqrt(jnp.float32(GENES)) * product(zmat, final) / jnp.sqrt(total)

    def project(batch):
        return inner(batch.astype(jnp.float32), basis)
    projected = lax.map(project, batches).reshape(CELLS, ELL)
    spread = lax.optimization_barrier(jnp.sum(projected * projected, axis=0)) / jnp.float32(CELLS)
    scores = projected / jnp.sqrt(spread + 1e-05)
    return (basis, scores)
```

```python
import jax
import jax.numpy as jnp
from jax import lax
from jax.experimental import pallas as pl
from jax.experimental.pallas import tpu as pltpu
from jax.sharding import PartitionSpec as P

GENES = 20480
CELLS = 4096
ELL = 256
NS_ITERS = 8
NY, NX, NZ = 4, 4, 8
NYZ = NY * NZ
LOCAL = GENES // 16
QUART = LOCAL // NY
PART = LOCAL // 16
MESH = pl.DeviceIdType.MESH
F32 = jnp.float32
BF16 = jnp.bfloat16
NT = (((1,), (1,)), ((), ()))
NN = (((1,), (0,)), ((), ()))
TN = (((0,), (0,)), ((), ()))


def split(a):
    hi = a.astype(BF16)
    return hi, (a - hi.astype(F32)).astype(BF16)


def dot(a, b, dims):
    return lax.dot_general(a, b, dims, preferred_element_type=F32)


def dot2(a, b, dims):
    return dot(a, b[0], dims) + dot(a, b[1], dims)


def dot3(a, b, dims):
    return dot(a[0], b[0], dims) + (dot(a[0], b[1], dims) + dot(a[1], b[0], dims))


def joined(pair):
    return jnp.concatenate([pair[0], pair[1]], axis=1)


def halves(ref, block):
    ref[0] = block[:, :128]
    ref[1] = block[:, 128:]


def kernel(
    x_ref, mix_ref, basis_ref, scores_ref,
    xt, rx, part, corebuf, half, rsbuf, xbuf, total,
    selfp, selfcore, selfhalf, selfrs, selfall,
    low, high, quad, mid, pairbuf2, pairbuf3, pairself, final,
    gh, gl, fh, fl, prod, prodcore, prodhalf, prodrs, sq,
    send_sem, core_sem, rs_sem, ag_sem, cag_sem, x_sem,
    a2a_sem, self_sem, pair_sem, pself_sem, fin_sem, pr_sem, sq_sem,
):
    cell, gene = lax.axis_index("cell"), lax.axis_index("gene")
    x, y = cell // NY, cell % NY
    z, c = gene // 2, gene % 2
    yz = y * NZ + z
    sends = []

    def put(src, dst, send, recv, to):
        copy = pltpu.make_async_remote_copy(
            src_ref=src, dst_ref=dst, send_sem=send, recv_sem=recv,
            device_id=to, device_id_type=MESH,
        )
        copy.start()
        return copy

    def taken(like, sem):
        pltpu.make_async_copy(like, like, sem).wait()

    def sent(like, sem):
        sends.append((like, sem))

    def other(i):
        j = lax.rem(yz + i, NYZ)
        return j, (x * NY + j // NZ, (j % NZ) * 2 + c)

    sibling = (cell, z * 2 + (1 - c))

    barrier = pltpu.get_barrier_semaphore()

    def greet(to):
        pl.semaphore_signal(barrier, inc=1, device_id=to, device_id_type=MESH)

    def greet_yz(i, carry):
        greet(other(i)[1])
        return carry

    lax.fori_loop(1, NYZ, greet_yz, 0)

    def greet_cells(i, carry):
        greet((lax.rem(cell - y + NY * (1 + i // NY), 16) + i % NY, gene))
        return carry

    lax.fori_loop(0, 12, greet_cells, 0)
    greet(sibling)

    for t in range(LOCAL // 128):
        xt[t * 128:(t + 1) * 128, :] = x_ref[:, t * 128:(t + 1) * 128].astype(F32).T
    own = pl.ds(pl.multiple_of(y * QUART, QUART), QUART)
    rx[y] = xt[own, :]
    xb = x_ref[...]
    halves(selfp, dot(xb, xb, NT))
    pl.semaphore_wait(barrier, NYZ - 1 + 12 + 1)

    for i in range(1, NY):
        q = lax.rem(y + i, NY)
        put(
            xt.at[pl.ds(pl.multiple_of(q * QUART, QUART), QUART), :], rx.at[y],
            send_sem.at[0], a2a_sem, (x * NY + q, gene),
        )
    sent(xt.at[pl.ds(0, 3 * QUART), :], send_sem.at[0])

    def rows(base, count):
        return pl.ds(pl.multiple_of(base, count), count)

    mine = rows(c * 128, 128)
    theirs = rows((1 - c) * 128, 128)

    put(selfp.at[:, theirs, :], selfcore, send_sem.at[1], self_sem.at[0], sibling)
    sent(selfcore, send_sem.at[1])
    taken(selfcore, self_sem.at[0])
    selfhalf[...] = selfp[:, mine, :] + selfcore[...]
    for i in range(1, NZ):
        k = lax.rem(z + i, NZ)
        put(
            selfhalf.at[:, rows(k * 16, 16), :], selfrs.at[i - 1],
            send_sem.at[2], self_sem.at[1], (cell, k * 2 + c),
        )
    sent(selfrs, send_sem.at[2])
    taken(selfrs, self_sem.at[1])
    piece = selfhalf[:, rows(z * 16, 16), :]
    for i in range(NZ - 1):
        piece = piece + selfrs[i]
    place = rows(c * 128 + z * 16, 16)
    selfall[y, :, place, :] = piece
    for i in range(1, NZ):
        k = lax.rem(z + i, NZ)
        put(
            selfall.at[y, :, place, :], selfall.at[y, :, place, :],
            send_sem.at[3], self_sem.at[2], (cell, k * 2 + c),
        )
    sent(selfrs, send_sem.at[3])
    taken(selfrs, self_sem.at[2])
    for i in range(1, NY):
        q = lax.rem(y + i, NY)
        put(
            selfall.at[y, :, mine, :], selfall.at[y, :, mine, :],
            send_sem.at[4], self_sem.at[3], (x * NY + q, gene),
        )
    sent(selfall.at[pl.ds(0, 3), :, pl.ds(0, 128), :], send_sem.at[4])

    taken(rx.at[pl.ds(0, 3)], a2a_sem)

    def reduced(level, at, count, planes):
        block = pl.ds(at, count)
        sem = 5 + 5 * level
        put(
            part.at[block, :, theirs, :], corebuf.at[block],
            send_sem.at[sem], core_sem.at[level], sibling,
        )
        sent(corebuf.at[block], send_sem.at[sem])
        taken(corebuf.at[block], core_sem.at[level])
        half[block] = part[block, :, mine, :] + corebuf[block]

        def spread(i, carry):
            j, to = other(i)
            put(
                half.at[block, j // 16, rows((j % 16) * 8, 8), :], rsbuf.at[i - 1, block],
                send_sem.at[sem + 1], rs_sem.at[level], to,
            )
            return carry

        lax.fori_loop(1, NYZ, spread, 0)
        sent(rsbuf.at[:, block], send_sem.at[sem + 1])
        taken(rsbuf.at[:, block], rs_sem.at[level])
        tile = half[block, yz // 16, rows((yz % 16) * 8, 8), :]
        for i in range(NYZ - 1):
            tile = tile + rsbuf[i, block]
        if planes:
            slot = level - 2
            xbuf[slot, x] = tile
            for d in planes:
                to = (x // d % 2 * -2 * d + x + d) if len(planes) == 1 else lax.rem(x + d, NX)
                put(
                    xbuf.at[slot, x], xbuf.at[slot, x],
                    send_sem.at[sem + 2], x_sem.at[slot], (to * NY + y, gene),
                )
            sent(xbuf.at[slot, pl.ds(0, len(planes))], send_sem.at[sem + 2])
            taken(xbuf.at[slot, pl.ds(0, len(planes))], x_sem.at[slot])
            if len(planes) == 1:
                base = x - x % 2
                tile = xbuf[slot, base] + xbuf[slot, base + 1]
            else:
                tile = (xbuf[slot, 0] + xbuf[slot, 1]) + (xbuf[slot, 2] + xbuf[slot, 3])
        spot = rows(c * 128 + (yz % 16) * 8, 8)
        total[block, yz // 16, spot, :] = tile

        def collect(i, carry):
            _, to = other(i)
            piece = total.at[block, yz // 16, spot, :]
            put(piece, piece, send_sem.at[sem + 3], ag_sem.at[level], to)
            return carry

        lax.fori_loop(1, NYZ, collect, 0)
        sent(rsbuf.at[:, block], send_sem.at[sem + 3])
        taken(rsbuf.at[:, block], ag_sem.at[level])
        put(
            total.at[block, :, mine, :], total.at[block, :, mine, :],
            send_sem.at[sem + 4], cag_sem.at[level], sibling,
        )
        sent(corebuf.at[block], send_sem.at[sem + 4])
        taken(corebuf.at[block], cag_sem.at[level])

    def weights(level, lower, cross, upper):
        gram = jnp.concatenate(
            [
                jnp.concatenate([lower, cross], axis=1),
                jnp.concatenate([cross.T, upper], axis=1),
            ],
            axis=0,
        )
        inv = 1.0 / jnp.sqrt(jnp.sum(gram * gram, keepdims=True) + 1e-06)
        hi, lo = split(gram)
        gh[...] = hi
        gl[...] = lo
        mix = mix_ref[level]
        once = dot2(mix, (gh[...], gl[...]), NN)
        twice = dot3(split(once), (gh[...], gl[...]), NN)
        return 0.5 * mix.astype(F32) + once * inv - (0.5 * twice) * (inv * inv)

    def own_gram(w):
        return dot3(split(dot3(w, (gh[...], gl[...]), NN)), w, NT)

    def left(w):
        return w[0][:, :ELL], w[1][:, :ELL]

    def right(w):
        return w[0][:, ELL:], w[1][:, ELL:]

    for p in range(2):
        halves(part.at[p], dot(rx[2 * p].astype(BF16), rx[2 * p + 1].astype(BF16), TN))
    reduced(0, 0, 2, ())
    taken(selfall.at[pl.ds(0, 3), :, pl.ds(0, 128), :], self_sem.at[3])
    put(
        selfall.at[:, :, mine, :], selfall.at[:, :, mine, :],
        send_sem.at[25], self_sem.at[4], sibling,
    )
    sent(selfall.at[:, :, pl.ds(0, 128), :], send_sem.at[25])
    taken(selfall.at[:, :, pl.ds(0, 128), :], self_sem.at[4])
    grams = []
    for p, sketch in ((0, low), (1, high)):
        w = split(weights(0, joined(selfall[2 * p]), joined(total[p]), joined(selfall[2 * p + 1])))
        sketch[...] = dot2(rx[2 * p].astype(BF16), left(w), NT) + dot2(
            rx[2 * p + 1].astype(BF16), right(w), NT
        )
        grams.append(own_gram(w))

    lows, highs = split(low[...]), split(high[...])
    halves(part.at[2], dot3(lows, highs, TN))
    reduced(1, 2, 1, ())
    w = split(weights(1, grams[0], joined(total[2]), grams[1]))
    quad[...] = dot3(lows, left(w), NT) + dot3(highs, right(w), NT)

    for level, step, src, buf, out in ((2, 1, quad, pairbuf2, mid), (3, 2, mid, pairbuf3, None)):
        slot = level - 2
        bit = x // step % 2
        to = ((x + step * (1 - 2 * bit)) * NY + y, gene)
        count = buf.shape[1]
        put(
            src.at[rows((1 - bit) * count, count), :], buf.at[bit],
            send_sem.at[26 + slot], pair_sem.at[slot], to,
        )
        sent(buf.at[0], send_sem.at[26 + slot])
        buf[bit] = src[rows(bit * count, count), :]
        halves(pairself.at[slot, bit], own_gram(w))
        share = pairself.at[slot, bit, :, mine, :]
        put(share, share, send_sem.at[28 + slot], pself_sem.at[slot], to)
        sent(pairself.at[slot, 0, :, pl.ds(0, 128), :], send_sem.at[28 + slot])
        taken(buf.at[0], pair_sem.at[slot])
        lows, highs = split(buf[0]), split(buf[1])
        halves(part.at[level + 1], dot3(lows, highs, TN))
        reduced(level, level + 1, 1, (1,) if level == 2 else (1, 2, 3))
        taken(pairself.at[slot, 0, :, pl.ds(0, 128), :], pself_sem.at[slot])
        across = pairself.at[slot, 1 - bit, :, mine, :]
        put(across, across, send_sem.at[30 + slot], pself_sem.at[2 + slot], sibling)
        sent(pairself.at[slot, 0, :, pl.ds(0, 128), :], send_sem.at[30 + slot])
        taken(pairself.at[slot, 0, :, pl.ds(0, 128), :], pself_sem.at[2 + slot])
        w = split(
            weights(
                level, joined(pairself[slot, 0]), joined(total[level + 1]), joined(pairself[slot, 1])
            )
        )
        sketch = dot3(lows, left(w), NT) + dot3(highs, right(w), NT)
        if out is not None:
            out[...] = sketch

    start = y * QUART + x % 2 * (2 * PART) + x // 2 * PART
    here = final.at[rows(start, PART), :]
    final[rows(start, PART), :] = sketch
    for i in range(1, 16):
        put(here, here, send_sem.at[32], fin_sem, (lax.rem(cell + i, 16), gene))
    sent(final.at[pl.ds(0, 15 * PART), :], send_sem.at[32])

    gram = own_gram(w)
    norm = jnp.sqrt(jnp.sum(gram * gram, keepdims=True) + 1e-06)
    eye = (
        lax.broadcasted_iota(jnp.int32, (ELL, ELL), 0) == lax.broadcasted_iota(jnp.int32, (ELL, ELL), 1)
    ).astype(F32)
    ymat = gram * (1.0 / norm)
    middle = 1.5 * eye - 0.5 * ymat
    zmat = middle
    ymat = dot3(split(ymat), split(middle), NN)

    def refine(step, carry):
        ymat, zmat = split(carry[0]), split(carry[1])
        middle = split(1.5 * eye - 0.5 * dot3(zmat, ymat, NN))
        return dot3(ymat, middle, NN), dot3(middle, zmat, NN)

    ymat, zmat = lax.fori_loop(0, NS_ITERS - 2, refine, (ymat, zmat))
    ymat, zmat = split(ymat), split(zmat)
    middle = split(1.5 * eye - 0.5 * dot3(zmat, ymat, NN))
    scaled = split(dot3(middle, zmat, NN) * (jnp.sqrt(F32(GENES)) / jnp.sqrt(norm)))

    taken(final.at[pl.ds(0, 15 * PART), :], fin_sem)
    hi, lo = split(final[...])
    fh[...] = hi
    fl[...] = lo
    shares = dot2(x_ref[...], (fh[...], fl[...]), NN)
    prod[...] = dot3(scaled, split(shares), NT).reshape(NZ, 2, 16, ELL)

    put(prod.at[:, 1 - c], prodcore, send_sem.at[33], pr_sem.at[0], sibling)
    sent(prodcore, send_sem.at[33])
    taken(prodcore, pr_sem.at[0])
    prodhalf[...] = prod[:, c] + prodcore[...]
    for i in range(1, NZ):
        k = lax.rem(z + i, NZ)
        put(prodhalf.at[k], prodrs.at[i - 1], send_sem.at[34], pr_sem.at[1], (cell, k * 2 + c))
    sent(prodrs, send_sem.at[34])
    basis_ref[...] = dot3(scaled, (fh[...], fl[...]), NT)
    taken(prodrs, pr_sem.at[1])
    scores = prodhalf[z]
    for i in range(NZ - 1):
        scores = scores + prodrs[i]
    sq[cell] = jnp.broadcast_to(jnp.sum(scores * scores, axis=1, keepdims=True), (16, 128))
    for i in range(1, 16):
        put(sq.at[cell], sq.at[cell], send_sem.at[35], sq_sem, (lax.rem(cell + i, 16), gene))
    sent(sq.at[pl.ds(0, 15)], send_sem.at[35])
    taken(sq.at[pl.ds(0, 15)], sq_sem)
    spread = jnp.sum(sq[...], axis=0)[:, :1] * (1.0 / CELLS)
    scores_ref[...] = (scores / jnp.sqrt(spread + 1e-05)).T
    for like, sem in sends:
        taken(like, sem)


def on_device(expression, mixing):
    vmem = pl.BlockSpec(memory_space=pltpu.VMEM)
    dma = pltpu.SemaphoreType.DMA

    def buf(*shape, kind=F32):
        return pltpu.VMEM(shape, kind)

    return pl.pallas_call(
        kernel,
        out_shape=(
            jax.ShapeDtypeStruct((ELL, LOCAL), F32),
            jax.ShapeDtypeStruct((ELL, 16), F32),
        ),
        in_specs=[vmem, vmem],
        out_specs=(vmem, vmem),
        scratch_shapes=[
            buf(LOCAL, ELL), buf(NY, QUART, ELL), buf(5, 2, 256, 128), buf(5, 2, 128, 128),
            buf(5, 2, 128, 128), buf(NYZ - 1, 5, 8, 128), buf(2, NX, 1, 8, 128), buf(5, 2, 256, 128),
            buf(2, 256, 128), buf(2, 128, 128), buf(2, 128, 128), buf(NZ - 1, 2, 16, 128),
            buf(NY, 2, 256, 128),
            buf(QUART, ELL), buf(QUART, ELL), buf(QUART, ELL), buf(2 * PART, ELL),
            buf(2, 2 * PART, ELL), buf(2, PART, ELL), buf(2, 2, 2, 256, 128), buf(LOCAL, ELL),
            buf(2 * ELL, 2 * ELL, kind=BF16), buf(2 * ELL, 2 * ELL, kind=BF16),
            buf(LOCAL, ELL, kind=BF16), buf(LOCAL, ELL, kind=BF16),
            buf(NZ, 2, 16, ELL), buf(NZ, 16, ELL), buf(NZ, 16, ELL), buf(NZ - 1, 16, ELL),
            buf(16, 16, 128),
            dma((36,)), dma((4,)), dma((4,)), dma((4,)), dma((4,)), dma((2,)),
            dma, dma((5,)), dma((2,)), dma((4,)), dma, dma((2,)), dma,
        ],
        compiler_params=pltpu.CompilerParams(
            collective_id=0, has_side_effects=True, vmem_limit_bytes=52 * 2**20
        ),
    )(expression, mixing)


def solution(mesh):
    return jax.shard_map(
        on_device,
        mesh=mesh,
        in_specs=(P("cell", "gene"), P()),
        out_specs=(P(None, "gene"), P("cell", "gene")),
        check_vma=False,
    )
```

```python
import jax
import jax.numpy as jnp
from jax import lax
from jax.experimental import pallas as pl
from jax.experimental.pallas import tpu as pltpu
from jax.sharding import PartitionSpec as P

GENES = 20480
CELLS = 4096
ELL = 256
NS_ITERS = 8
NY, NX, NZ = 4, 4, 8
NYZ = NY * NZ
LOCAL = GENES // 16
QUART = LOCAL // NY
PART = LOCAL // 16
MESH = pl.DeviceIdType.MESH
F32 = jnp.float32
BF16 = jnp.bfloat16
NT = (((1,), (1,)), ((), ()))
NN = (((1,), (0,)), ((), ()))
TN = (((0,), (0,)), ((), ()))


def hops(d, n):
    return min(d, n - d)


ALONG_Y = sorted(range(1, NY), key=lambda d: -hops(d, NY))
ALONG_Z = sorted(range(1, NZ), key=lambda d: -hops(d, NZ))
OTHERS = sorted(
    ((dy, dz) for dy in range(NY) for dz in range(NZ) if dy or dz),
    key=lambda d: -hops(d[0], NY) - hops(d[1], NZ),
)
PLANES = {
    2: sorted(
        ((dx, dy) for dx in range(2) for dy in range(NY) if dx or dy),
        key=lambda d: -d[0] - hops(d[1], NY),
    ),
    3: sorted(
        ((dx, dy) for dx in range(NX) for dy in range(NY) if dx or dy),
        key=lambda d: -hops(d[0], NX) - hops(d[1], NY),
    ),
}


def split(a):
    hi = a.astype(BF16)
    return hi, (a - hi.astype(F32)).astype(BF16)


def dot(a, b, dims):
    return lax.dot_general(a, b, dims, preferred_element_type=F32)


def dot2(a, b, dims):
    return dot(a, b[0], dims) + dot(a, b[1], dims)


def dot3(a, b, dims):
    return dot(a[0], b[0], dims) + (dot(a[0], b[1], dims) + dot(a[1], b[0], dims))


def joined(pair):
    return jnp.concatenate([pair[0], pair[1]], axis=1)


def halves(ref, block):
    ref[0] = block[:, :128]
    ref[1] = block[:, 128:]


def kernel(
    x_hbm, mix_hbm, basis_ref, scores_ref,
    x_ref, mix_ref, xt, rx, part, corebuf, half, rsbuf, cellbuf, zbuf, total,
    selfp, selfcore, selfhalf, selfrs, selfall,
    low, high, quad, mid, pairbuf2, pairbuf3, pairself, final,
    gh, gl, fh, fl, prod, prodcore, prodhalf, prodrs, sq,
    load_sem, send_sem, core_sem, rs_sem, ag_sem, cag_sem, z_sem,
    a2a_sem, self_sem, pair_sem, pself_sem, fin_sem, finx_sem, finy_sem, pr_sem, sq_sem,
):
    cell, gene = lax.axis_index("cell"), lax.axis_index("gene")
    x, y = cell // NY, cell % NY
    z, c = gene // 2, gene % 2
    yz = y * NZ + z
    sends = []

    def put(src, dst, send, recv, to):
        copy = pltpu.make_async_remote_copy(
            src_ref=src, dst_ref=dst, send_sem=send, recv_sem=recv,
            device_id=to, device_id_type=MESH,
        )
        copy.start()
        return copy

    def taken(like, sem):
        pltpu.make_async_copy(like, like, sem).wait()

    def sent(like, sem):
        sends.append((like, sem))

    def at(dx, dy, dz):
        return (lax.rem(x + dx, NX) * NY + lax.rem(y + dy, NY), lax.rem(z + dz, NZ) * 2 + c)

    def paired(dx, dy):
        return ((x + dx * (1 - 2 * (x % 2))) * NY + lax.rem(y + dy, NY), gene)

    load_x = pltpu.make_async_copy(x_hbm, x_ref, load_sem.at[0])
    load_mix = pltpu.make_async_copy(mix_hbm, mix_ref, load_sem.at[1])
    load_x.start()
    load_mix.start()
    sibling = (cell, z * 2 + (1 - c))

    barrier = pltpu.get_barrier_semaphore()

    def greet(to):
        pl.semaphore_signal(barrier, inc=1, device_id=to, device_id_type=MESH)

    for dy, dz in OTHERS:
        greet(at(0, dy, dz))
    for dx, dy in PLANES[3]:
        if dx:
            greet(at(dx, dy, 0))
    greet(sibling)
    load_x.wait()

    for t in range(LOCAL // 128):
        xt[t * 128:(t + 1) * 128, :] = x_ref[:, t * 128:(t + 1) * 128].astype(F32).T
    own = pl.ds(pl.multiple_of(y * QUART, QUART), QUART)
    rx[y] = xt[own, :]
    xb = x_ref[...]
    halves(selfp, dot(xb, xb, NT))
    pl.semaphore_wait(barrier, NYZ - 1 + 12 + 1)

    for i in ALONG_Y:
        q = lax.rem(y + i, NY)
        put(
            xt.at[pl.ds(pl.multiple_of(q * QUART, QUART), QUART), :], rx.at[y],
            send_sem.at[0], a2a_sem, (x * NY + q, gene),
        )
    sent(xt.at[pl.ds(0, 3 * QUART), :], send_sem.at[0])

    def rows(base, count):
        return pl.ds(pl.multiple_of(base, count), count)

    mine = rows(c * 128, 128)
    theirs = rows((1 - c) * 128, 128)

    put(selfp.at[:, theirs, :], selfcore, send_sem.at[1], self_sem.at[0], sibling)
    sent(selfcore, send_sem.at[1])
    taken(selfcore, self_sem.at[0])
    selfhalf[...] = selfp[:, mine, :] + selfcore[...]
    for i in ALONG_Z:
        k = lax.rem(z + i, NZ)
        put(
            selfhalf.at[:, rows(k * 16, 16), :], selfrs.at[i - 1],
            send_sem.at[2], self_sem.at[1], (cell, k * 2 + c),
        )
    sent(selfrs, send_sem.at[2])
    taken(selfrs, self_sem.at[1])
    piece = selfhalf[:, rows(z * 16, 16), :]
    for i in range(NZ - 1):
        piece = piece + selfrs[i]
    place = rows(c * 128 + z * 16, 16)
    selfall[y, :, place, :] = piece
    for i in ALONG_Z:
        k = lax.rem(z + i, NZ)
        put(
            selfall.at[y, :, place, :], selfall.at[y, :, place, :],
            send_sem.at[3], self_sem.at[2], (cell, k * 2 + c),
        )
    sent(selfrs, send_sem.at[3])
    taken(selfrs, self_sem.at[2])
    for i in ALONG_Y:
        q = lax.rem(y + i, NY)
        put(
            selfall.at[y, :, mine, :], selfall.at[y, :, mine, :],
            send_sem.at[4], self_sem.at[3], (x * NY + q, gene),
        )
    sent(selfall.at[pl.ds(0, 3), :, pl.ds(0, 128), :], send_sem.at[4])

    taken(rx.at[pl.ds(0, 3)], a2a_sem)

    def reduced(level, at_block, count):
        block = pl.ds(at_block, count)
        sem = 5 + 5 * level
        put(
            part.at[block, :, theirs, :], corebuf.at[block],
            send_sem.at[sem], core_sem.at[level], sibling,
        )
        sent(corebuf.at[block], send_sem.at[sem])
        taken(corebuf.at[block], core_sem.at[level])
        half[block] = part[block, :, mine, :] + corebuf[block]
        if level < 2:
            for dy, dz in OTHERS:
                k = lax.rem(y + dy, NY) * NZ + lax.rem(z + dz, NZ)
                put(
                    half.at[block, k // 16, rows((k % 16) * 8, 8), :],
                    rsbuf.at[dy * NZ + dz - 1, block],
                    send_sem.at[sem + 1], rs_sem.at[level], at(0, dy, dz),
                )
            sent(rsbuf.at[:, block], send_sem.at[sem + 1])
            taken(rsbuf.at[:, block], rs_sem.at[level])
            tile = half[block, yz // 16, rows((yz % 16) * 8, 8), :]
            for i in range(NYZ - 1):
                tile = tile + rsbuf[i, block]
            piece = total.at[block, yz // 16, rows(c * 128 + (yz % 16) * 8, 8), :]
            piece[...] = tile
            for dy, dz in OTHERS:
                put(piece, piece, send_sem.at[sem + 3], ag_sem.at[level], at(0, dy, dz))
            sent(rsbuf.at[:, block], send_sem.at[sem + 3])
            taken(rsbuf.at[:, block], ag_sem.at[level])
        else:
            slot = level - 2
            peers = PLANES[level]
            strip = 128 // (len(peers) + 1)
            inbox = cellbuf.at[slot, pl.ds(0, len(peers)), :, pl.ds(0, strip), :]
            whose = (lambda dx, dy: paired(dx, dy)) if level == 2 else (lambda dx, dy: at(dx, dy, 0))
            index = (lambda to: to % 8) if level == 2 else (lambda to: to)
            own = half[at_block, :, rows(index(cell) * strip, strip), :]
            for dx, dy in peers:
                to = whose(dx, dy)
                put(
                    half.at[at_block, :, rows(index(to[0]) * strip, strip), :],
                    cellbuf.at[slot, dx * NY + dy - 1, :, pl.ds(0, strip), :],
                    send_sem.at[sem + 1], rs_sem.at[level], to,
                )
            sent(inbox, send_sem.at[sem + 1])
            taken(inbox, rs_sem.at[level])
            for i in range(len(peers)):
                own = own + cellbuf[slot, i, :, :strip, :]
            share = zbuf.at[slot, z, :, pl.ds(0, strip), :]
            share[...] = own
            for dz in ALONG_Z:
                put(share, share, send_sem.at[sem + 2], z_sem.at[slot], at(0, 0, dz))
            inbox = zbuf.at[slot, pl.ds(0, NZ - 1), :, pl.ds(0, strip), :]
            sent(inbox, send_sem.at[sem + 2])
            taken(inbox, z_sem.at[slot])
            own = zbuf[slot, 0, :, :strip, :]
            for i in range(1, NZ):
                own = own + zbuf[slot, i, :, :strip, :]
            piece = total.at[at_block, :, rows(c * 128 + index(cell) * strip, strip), :]
            piece[...] = own
            for dx, dy in peers:
                put(piece, piece, send_sem.at[sem + 3], ag_sem.at[level], whose(dx, dy))
            inbox = cellbuf.at[slot, pl.ds(0, len(peers)), :, pl.ds(0, strip), :]
            sent(inbox, send_sem.at[sem + 3])
            taken(inbox, ag_sem.at[level])
        put(
            total.at[block, :, mine, :], total.at[block, :, mine, :],
            send_sem.at[sem + 4], cag_sem.at[level], sibling,
        )
        sent(corebuf.at[block], send_sem.at[sem + 4])
        taken(corebuf.at[block], cag_sem.at[level])

    def weights(level, lower, cross, upper):
        gram = jnp.concatenate(
            [
                jnp.concatenate([lower, cross], axis=1),
                jnp.concatenate([cross.T, upper], axis=1),
            ],
            axis=0,
        )
        inv = 1.0 / jnp.sqrt(jnp.sum(gram * gram, keepdims=True) + 1e-06)
        hi, lo = split(gram)
        gh[...] = hi
        gl[...] = lo
        mix = mix_ref[level]
        once = dot2(mix, (gh[...], gl[...]), NN)
        twice = dot3(split(once), (gh[...], gl[...]), NN)
        return 0.5 * mix.astype(F32) + once * inv - (0.5 * twice) * (inv * inv)

    def own_gram(w):
        return dot3(split(dot3(w, (gh[...], gl[...]), NN)), w, NT)

    def left(w):
        return w[0][:, :ELL], w[1][:, :ELL]

    def right(w):
        return w[0][:, ELL:], w[1][:, ELL:]

    for p in range(2):
        halves(part.at[p], dot(rx[2 * p].astype(BF16), rx[2 * p + 1].astype(BF16), TN))
    reduced(0, 0, 2)
    load_mix.wait()
    taken(selfall.at[pl.ds(0, 3), :, pl.ds(0, 128), :], self_sem.at[3])
    put(
        selfall.at[:, :, mine, :], selfall.at[:, :, mine, :],
        send_sem.at[25], self_sem.at[4], sibling,
    )
    sent(selfall.at[:, :, pl.ds(0, 128), :], send_sem.at[25])
    taken(selfall.at[:, :, pl.ds(0, 128), :], self_sem.at[4])
    grams = []
    for p, sketch in ((0, low), (1, high)):
        w = split(weights(0, joined(selfall[2 * p]), joined(total[p]), joined(selfall[2 * p + 1])))
        sketch[...] = dot2(rx[2 * p].astype(BF16), left(w), NT) + dot2(
            rx[2 * p + 1].astype(BF16), right(w), NT
        )
        grams.append(own_gram(w))

    lows, highs = split(low[...]), split(high[...])
    halves(part.at[2], dot3(lows, highs, TN))
    reduced(1, 2, 1)
    w = split(weights(1, grams[0], joined(total[2]), grams[1]))
    quad[...] = dot3(lows, left(w), NT) + dot3(highs, right(w), NT)

    for level, step, src, buf, out in ((2, 1, quad, pairbuf2, mid), (3, 2, mid, pairbuf3, None)):
        slot = level - 2
        bit = x // step % 2
        to = ((x + step * (1 - 2 * bit)) * NY + y, gene)
        count = buf.shape[1]
        put(
            src.at[rows((1 - bit) * count, count), :], buf.at[bit],
            send_sem.at[26 + slot], pair_sem.at[slot], to,
        )
        sent(buf.at[0], send_sem.at[26 + slot])
        buf[bit] = src[rows(bit * count, count), :]
        halves(pairself.at[slot, bit], own_gram(w))
        share = pairself.at[slot, bit, :, mine, :]
        put(share, share, send_sem.at[28 + slot], pself_sem.at[slot], to)
        sent(pairself.at[slot, 0, :, pl.ds(0, 128), :], send_sem.at[28 + slot])
        taken(buf.at[0], pair_sem.at[slot])
        lows, highs = split(buf[0]), split(buf[1])
        halves(part.at[level + 1], dot3(lows, highs, TN))
        reduced(level, level + 1, 1)
        taken(pairself.at[slot, 0, :, pl.ds(0, 128), :], pself_sem.at[slot])
        across = pairself.at[slot, 1 - bit, :, mine, :]
        put(across, across, send_sem.at[30 + slot], pself_sem.at[2 + slot], sibling)
        sent(pairself.at[slot, 0, :, pl.ds(0, 128), :], send_sem.at[30 + slot])
        taken(pairself.at[slot, 0, :, pl.ds(0, 128), :], pself_sem.at[2 + slot])
        w = split(
            weights(
                level, joined(pairself[slot, 0]), joined(total[level + 1]), joined(pairself[slot, 1])
            )
        )
        sketch = dot3(lows, left(w), NT) + dot3(highs, right(w), NT)
        if out is not None:
            out[...] = sketch

    def chunk(cx, cy, part_of=0, count=PART):
        return final.at[rows(cy * QUART + cx % 2 * (2 * PART) + cx // 2 * PART + part_of, count), :]

    here = chunk(x, y)
    here[...] = sketch
    for d in ALONG_Y:
        put(here, here, send_sem.at[32], finx_sem.at[d - 1], at(d, 0, 0))
        put(here, here, send_sem.at[32], finy_sem.at[d - 1], at(0, d, 0))
    sent(final.at[pl.ds(0, 15 * PART), :], send_sem.at[32])
    for d in (1, 3, 2):
        cx, cy = lax.rem(x + NX - d, NX), lax.rem(y + NY - d, NY)
        taken(here, finx_sem.at[d - 1])
        first = chunk(cx, y, 0, PART // 2)
        for e in ALONG_Y:
            put(first, first, send_sem.at[32], fin_sem, at(0, e, 0))
        taken(here, finy_sem.at[d - 1])
        second = chunk(x, cy, PART // 2, PART // 2)
        for e in ALONG_Y:
            put(second, second, send_sem.at[32], fin_sem, at(e, 0, 0))

    gram = own_gram(w)
    norm = jnp.sqrt(jnp.sum(gram * gram, keepdims=True) + 1e-06)
    eye = (
        lax.broadcasted_iota(jnp.int32, (ELL, ELL), 0) == lax.broadcasted_iota(jnp.int32, (ELL, ELL), 1)
    ).astype(F32)
    ymat = gram * (1.0 / norm)
    middle = 1.5 * eye - 0.5 * ymat
    zmat = middle
    ymat = dot3(split(ymat), split(middle), NN)

    def refine(step, carry):
        ymat, zmat = split(carry[0]), split(carry[1])
        middle = split(1.5 * eye - 0.5 * dot3(zmat, ymat, NN))
        return dot3(ymat, middle, NN), dot3(middle, zmat, NN)

    ymat, zmat = lax.fori_loop(0, NS_ITERS - 2, refine, (ymat, zmat))
    ymat, zmat = split(ymat), split(zmat)
    middle = split(1.5 * eye - 0.5 * dot3(zmat, ymat, NN))
    scaled = split(dot3(middle, zmat, NN) * (jnp.sqrt(F32(GENES)) / jnp.sqrt(norm)))

    taken(final.at[pl.ds(0, 9 * PART), :], fin_sem)
    hi, lo = split(final[...])
    fh[...] = hi
    fl[...] = lo
    shares = dot2(x_ref[...], (fh[...], fl[...]), NN)
    prod[...] = dot3(scaled, split(shares), NT).reshape(NZ, 2, 16, ELL)

    put(prod.at[:, 1 - c], prodcore, send_sem.at[33], pr_sem.at[0], sibling)
    sent(prodcore, send_sem.at[33])
    taken(prodcore, pr_sem.at[0])
    prodhalf[...] = prod[:, c] + prodcore[...]
    for i in ALONG_Z:
        k = lax.rem(z + i, NZ)
        put(prodhalf.at[k], prodrs.at[i - 1], send_sem.at[34], pr_sem.at[1], (cell, k * 2 + c))
    sent(prodrs, send_sem.at[34])
    basis_ref[...] = dot3(scaled, (fh[...], fl[...]), NT)
    taken(prodrs, pr_sem.at[1])
    scores = prodhalf[z]
    for i in range(NZ - 1):
        scores = scores + prodrs[i]
    sq[cell] = jnp.broadcast_to(jnp.sum(scores * scores, axis=1, keepdims=True), (16, 128))
    for dx, dy in PLANES[3]:
        put(sq.at[cell], sq.at[cell], send_sem.at[35], sq_sem, at(dx, dy, 0))
    sent(sq.at[pl.ds(0, 15)], send_sem.at[35])
    taken(sq.at[pl.ds(0, 15)], sq_sem)
    spread = jnp.sum(sq[...], axis=0)[:, :1] * (1.0 / CELLS)
    scores_ref[...] = scores / jnp.sqrt(spread + 1e-05)
    for like, sem in sends:
        taken(like, sem)


def on_device(expression, mixing):
    vmem = pl.BlockSpec(memory_space=pltpu.VMEM)
    dma = pltpu.SemaphoreType.DMA

    def buf(*shape, kind=F32):
        return pltpu.VMEM(shape, kind)

    basis, scores = pl.pallas_call(
        kernel,
        out_shape=(
            jax.ShapeDtypeStruct((ELL, LOCAL), F32),
            jax.ShapeDtypeStruct((16, ELL), F32),
        ),
        in_specs=[pl.BlockSpec(memory_space=pltpu.HBM)] * 2,
        out_specs=(vmem, vmem),
        scratch_shapes=[
            buf(ELL, LOCAL, kind=BF16), buf(4, ELL, 2 * ELL, kind=BF16),
            buf(LOCAL, ELL), buf(NY, QUART, ELL), buf(5, 2, 256, 128), buf(5, 2, 128, 128),
            buf(5, 2, 128, 128), buf(NYZ - 1, 5, 8, 128), buf(2, 15, 2, 16, 128), buf(2, NZ, 2, 16, 128), buf(5, 2, 256, 128),
            buf(2, 256, 128), buf(2, 128, 128), buf(2, 128, 128), buf(NZ - 1, 2, 16, 128),
            buf(NY, 2, 256, 128),
            buf(QUART, ELL), buf(QUART, ELL), buf(QUART, ELL), buf(2 * PART, ELL),
            buf(2, 2 * PART, ELL), buf(2, PART, ELL), buf(2, 2, 2, 256, 128), buf(LOCAL, ELL),
            buf(2 * ELL, 2 * ELL, kind=BF16), buf(2 * ELL, 2 * ELL, kind=BF16),
            buf(LOCAL, ELL, kind=BF16), buf(LOCAL, ELL, kind=BF16),
            buf(NZ, 2, 16, ELL), buf(NZ, 16, ELL), buf(NZ, 16, ELL), buf(NZ - 1, 16, ELL),
            buf(16, 16, 128),
            dma((2,)), dma((36,)), dma((4,)), dma((4,)), dma((4,)), dma((4,)), dma((2,)),
            dma, dma((5,)), dma((2,)), dma((4,)), dma, dma((3,)), dma((3,)), dma((2,)), dma,
        ],
        compiler_params=pltpu.CompilerParams(
            collective_id=0, has_side_effects=True, vmem_limit_bytes=28 * 2**20
        ),
    )(expression, mixing)
    return basis, scores.T


def solution(mesh):
    return jax.shard_map(
        on_device,
        mesh=mesh,
        in_specs=(P("cell", "gene"), P()),
        out_specs=(P(None, "gene"), P("cell", "gene")),
        check_vma=False,
    )
```

```python
import jax
import jax.numpy as jnp
from jax import lax
from jax.experimental import pallas as pl
from jax.experimental.pallas import tpu as pltpu
from jax.sharding import PartitionSpec as P

GENES = 20480
CELLS = 4096
ELL = 256
NS_ITERS = 8
NY, NX, NZ = 4, 4, 8
NYZ = NY * NZ
LOCAL = GENES // 16
QUART = LOCAL // NY
PART = LOCAL // 16
EARLY = PART // 2
MESH = pl.DeviceIdType.MESH
F32 = jnp.float32
BF16 = jnp.bfloat16
NT = (((1,), (1,)), ((), ()))
NN = (((1,), (0,)), ((), ()))
TN = (((0,), (0,)), ((), ()))


def hops(d, n):
    return min(d, n - d)


ALONG_Y = sorted(range(1, NY), key=lambda d: -hops(d, NY))
ALONG_Z = sorted(range(1, NZ), key=lambda d: -hops(d, NZ))
OTHERS = sorted(
    ((dy, dz) for dy in range(NY) for dz in range(NZ) if dy or dz),
    key=lambda d: -hops(d[0], NY) - hops(d[1], NZ),
)
PLANES = {
    2: sorted(
        ((dx, dy) for dx in range(2) for dy in range(NY) if dx or dy),
        key=lambda d: -d[0] - hops(d[1], NY),
    ),
    3: sorted(
        ((dx, dy) for dx in range(NX) for dy in range(NY) if dx or dy),
        key=lambda d: -hops(d[0], NX) - hops(d[1], NY),
    ),
}


def split(a):
    hi = a.astype(BF16)
    return hi, (a - hi.astype(F32)).astype(BF16)


def dot(a, b, dims):
    return lax.dot_general(a, b, dims, preferred_element_type=F32)


def dot2(a, b, dims):
    return dot(a, b[0], dims) + dot(a, b[1], dims)


def dot3(a, b, dims):
    return dot(a[0], b[0], dims) + (dot(a[0], b[1], dims) + dot(a[1], b[0], dims))


def joined(pair):
    return jnp.concatenate([pair[0], pair[1]], axis=1)


def halves(ref, block):
    ref[0] = block[:, :128]
    ref[1] = block[:, 128:]


def kernel(
    x_hbm, mix_hbm, basis_hbm, scores_ref,
    x_ref, mix_ref, basis_ref, xt, rx, part, corebuf, half, rsbuf, cellbuf, zbuf, total,
    selfp, selfcore, selfhalf, selfrs, selfall,
    low, high, quad, mid, pairbuf2, pairbuf3, pairself, early, final,
    gh, gl, fh, fl, prod, prodcore, prodhalf, prodrs, sq,
    load_sem, send_sem, core_sem, rs_sem, ag_sem, cag_sem, z_sem,
    a2a_sem, self_sem, pair_sem, pself_sem, earlyx_sem, earlyy_sem, early_sem, fin_sem, finx_sem, finy_sem, pr_sem, sq_sem,
):
    cell, gene = lax.axis_index("cell"), lax.axis_index("gene")
    x, y = cell // NY, cell % NY
    z, c = gene // 2, gene % 2
    yz = y * NZ + z
    sends = []

    def put(src, dst, send, recv, to):
        copy = pltpu.make_async_remote_copy(
            src_ref=src, dst_ref=dst, send_sem=send, recv_sem=recv,
            device_id=to, device_id_type=MESH,
        )
        copy.start()
        return copy

    def taken(like, sem):
        pltpu.make_async_copy(like, like, sem).wait()

    def sent(like, sem):
        sends.append((like, sem))

    def at(dx, dy, dz):
        return (lax.rem(x + dx, NX) * NY + lax.rem(y + dy, NY), lax.rem(z + dz, NZ) * 2 + c)

    def paired(dx, dy):
        return ((x + dx * (1 - 2 * (x % 2))) * NY + lax.rem(y + dy, NY), gene)

    load_x = pltpu.make_async_copy(x_hbm, x_ref, load_sem.at[0])
    load_mix = pltpu.make_async_copy(mix_hbm, mix_ref, load_sem.at[1])
    load_x.start()
    load_mix.start()
    sibling = (cell, z * 2 + (1 - c))

    barrier = pltpu.get_barrier_semaphore()

    def greet(to):
        pl.semaphore_signal(barrier, inc=1, device_id=to, device_id_type=MESH)

    for d in ALONG_Y:
        greet(at(0, d, 0))
    for d in ALONG_Z:
        greet(at(0, 0, d))
    for d in ALONG_Y:
        greet(at(d, 0, 0))
    greet(sibling)
    load_x.wait()

    for t in range(LOCAL // 128):
        xt[t * 128:(t + 1) * 128, :] = x_ref[:, t * 128:(t + 1) * 128].astype(F32).T
    own = pl.ds(pl.multiple_of(y * QUART, QUART), QUART)
    rx[y] = xt[own, :]
    xb = x_ref[...]
    halves(selfp, dot(xb, xb, NT))
    pl.semaphore_wait(barrier, NZ - 1 + NY - 1 + NX - 1 + 1)

    for i in ALONG_Y:
        q = lax.rem(y + i, NY)
        put(
            xt.at[pl.ds(pl.multiple_of(q * QUART, QUART), QUART), :], rx.at[y],
            send_sem.at[0], a2a_sem, (x * NY + q, gene),
        )
    sent(xt.at[pl.ds(0, 3 * QUART), :], send_sem.at[0])

    def rows(base, count):
        return pl.ds(pl.multiple_of(base, count), count)

    mine = rows(c * 128, 128)
    theirs = rows((1 - c) * 128, 128)

    put(selfp.at[:, theirs, :], selfcore, send_sem.at[1], self_sem.at[0], sibling)
    sent(selfcore, send_sem.at[1])
    taken(selfcore, self_sem.at[0])
    selfhalf[...] = selfp[:, mine, :] + selfcore[...]
    for i in ALONG_Z:
        k = lax.rem(z + i, NZ)
        put(
            selfhalf.at[:, rows(k * 16, 16), :], selfrs.at[i - 1],
            send_sem.at[2], self_sem.at[1], (cell, k * 2 + c),
        )
    sent(selfrs, send_sem.at[2])
    taken(selfrs, self_sem.at[1])
    piece = selfhalf[:, rows(z * 16, 16), :]
    for i in range(NZ - 1):
        piece = piece + selfrs[i]
    place = rows(c * 128 + z * 16, 16)
    selfall[y, :, place, :] = piece
    for i in ALONG_Z:
        k = lax.rem(z + i, NZ)
        put(
            selfall.at[y, :, place, :], selfall.at[y, :, place, :],
            send_sem.at[3], self_sem.at[2], (cell, k * 2 + c),
        )
    sent(selfrs, send_sem.at[3])
    taken(selfrs, self_sem.at[2])
    for i in ALONG_Y:
        q = lax.rem(y + i, NY)
        put(
            selfall.at[y, :, mine, :], selfall.at[y, :, mine, :],
            send_sem.at[4], self_sem.at[3], (x * NY + q, gene),
        )
    sent(selfall.at[pl.ds(0, 3), :, pl.ds(0, 128), :], send_sem.at[4])

    taken(rx.at[pl.ds(0, 3)], a2a_sem)

    def reduced(level, at_block, count, scattering=None, summing=None, gathering=None):
        block = pl.ds(at_block, count)
        sem = 5 + 5 * level
        put(
            part.at[block, :, theirs, :], corebuf.at[block],
            send_sem.at[sem], core_sem.at[level], sibling,
        )
        sent(corebuf.at[block], send_sem.at[sem])
        taken(corebuf.at[block], core_sem.at[level])
        half[block] = part[block, :, mine, :] + corebuf[block]
        if level < 2:
            for dy, dz in OTHERS:
                k = lax.rem(y + dy, NY) * NZ + lax.rem(z + dz, NZ)
                put(
                    half.at[block, k // 16, rows((k % 16) * 8, 8), :],
                    rsbuf.at[dy * NZ + dz - 1, block],
                    send_sem.at[sem + 1], rs_sem.at[level], at(0, dy, dz),
                )
            sent(rsbuf.at[:, block], send_sem.at[sem + 1])
            if scattering is not None:
                scattering()
            taken(rsbuf.at[:, block], rs_sem.at[level])
            tile = half[block, yz // 16, rows((yz % 16) * 8, 8), :]
            for i in range(NYZ - 1):
                tile = tile + rsbuf[i, block]
            piece = total.at[block, yz // 16, rows(c * 128 + (yz % 16) * 8, 8), :]
            piece[...] = tile
            for dy, dz in OTHERS:
                put(piece, piece, send_sem.at[sem + 3], ag_sem.at[level], at(0, dy, dz))
            sent(rsbuf.at[:, block], send_sem.at[sem + 3])
            if gathering is not None:
                gathering()
            taken(rsbuf.at[:, block], ag_sem.at[level])
        else:
            slot = level - 2
            peers = PLANES[level]
            strip = 128 // (len(peers) + 1)
            inbox = cellbuf.at[slot, pl.ds(0, len(peers)), :, pl.ds(0, strip), :]
            whose = (lambda dx, dy: paired(dx, dy)) if level == 2 else (lambda dx, dy: at(dx, dy, 0))
            index = (lambda to: to % 8) if level == 2 else (lambda to: to)
            own = half[at_block, :, rows(index(cell) * strip, strip), :]
            for dx, dy in peers:
                to = whose(dx, dy)
                put(
                    half.at[at_block, :, rows(index(to[0]) * strip, strip), :],
                    cellbuf.at[slot, dx * NY + dy - 1, :, pl.ds(0, strip), :],
                    send_sem.at[sem + 1], rs_sem.at[level], to,
                )
            sent(inbox, send_sem.at[sem + 1])
            scattering()
            taken(inbox, rs_sem.at[level])
            for i in range(len(peers)):
                own = own + cellbuf[slot, i, :, :strip, :]
            share = zbuf.at[slot, z, :, pl.ds(0, strip), :]
            share[...] = own
            for dz in ALONG_Z:
                put(share, share, send_sem.at[sem + 2], z_sem.at[slot], at(0, 0, dz))
            inbox = zbuf.at[slot, pl.ds(0, NZ - 1), :, pl.ds(0, strip), :]
            sent(inbox, send_sem.at[sem + 2])
            if summing is not None:
                summing()
            taken(inbox, z_sem.at[slot])
            own = zbuf[slot, 0, :, :strip, :]
            for i in range(1, NZ):
                own = own + zbuf[slot, i, :, :strip, :]
            piece = total.at[at_block, :, rows(c * 128 + index(cell) * strip, strip), :]
            piece[...] = own
            for dx, dy in peers:
                put(piece, piece, send_sem.at[sem + 3], ag_sem.at[level], whose(dx, dy))
            inbox = cellbuf.at[slot, pl.ds(0, len(peers)), :, pl.ds(0, strip), :]
            sent(inbox, send_sem.at[sem + 3])
            gathering()
            taken(inbox, ag_sem.at[level])
        put(
            total.at[block, :, mine, :], total.at[block, :, mine, :],
            send_sem.at[sem + 4], cag_sem.at[level], sibling,
        )
        sent(corebuf.at[block], send_sem.at[sem + 4])
        taken(corebuf.at[block], cag_sem.at[level])

    def weights(level, lower, cross, upper, slot=0):
        gram = jnp.concatenate(
            [
                jnp.concatenate([lower, cross], axis=1),
                jnp.concatenate([cross.T, upper], axis=1),
            ],
            axis=0,
        )
        inv = 1.0 / jnp.sqrt(jnp.sum(gram * gram, keepdims=True) + 1e-06)
        hi, lo = split(gram)
        gh[slot] = hi
        gl[slot] = lo
        mix = mix_ref[level]
        once = dot2(mix, (gh[slot], gl[slot]), NN)
        twice = dot3(split(once), (gh[slot], gl[slot]), NN)
        return 0.5 * mix.astype(F32) + once * inv - (0.5 * twice) * (inv * inv)

    def own_gram(w, slot=0):
        return dot3(split(dot3(w, (gh[slot], gl[slot]), NN)), w, NT)

    def left(w):
        return w[0][:, :ELL], w[1][:, :ELL]

    def right(w):
        return w[0][:, ELL:], w[1][:, ELL:]

    for p in range(2):
        halves(part.at[p], dot(rx[2 * p].astype(BF16), rx[2 * p + 1].astype(BF16), TN))

    def swap_selves():
        taken(selfall.at[pl.ds(0, 3), :, pl.ds(0, 128), :], self_sem.at[3])
        put(
            selfall.at[:, :, mine, :], selfall.at[:, :, mine, :],
            send_sem.at[25], self_sem.at[4], sibling,
        )
        sent(selfall.at[:, :, pl.ds(0, 128), :], send_sem.at[25])

    reduced(0, 0, 2, gathering=swap_selves)
    load_mix.wait()
    taken(selfall.at[:, :, pl.ds(0, 128), :], self_sem.at[4])
    kept = []
    for p, sketch in ((0, low), (1, high)):
        w = split(weights(0, joined(selfall[2 * p]), joined(total[p]), joined(selfall[2 * p + 1]), p))
        sketch[...] = dot2(rx[2 * p].astype(BF16), left(w), NT) + dot2(
            rx[2 * p + 1].astype(BF16), right(w), NT
        )
        kept.append(w)

    lows, highs = split(low[...]), split(high[...])
    halves(part.at[2], dot3(lows, highs, TN))
    grams = []
    reduced(1, 2, 1, lambda: grams.extend(own_gram(kept[p], p) for p in range(2)))
    w = split(weights(1, grams[0], joined(total[2]), grams[1]))

    def order(cx, cy):
        return cy * 4 + cx % 2 * 2 + cx // 2

    for level, step, src, buf in ((2, 1, quad, pairbuf2), (3, 2, mid, pairbuf3)):
        slot = level - 2
        bit = x // step % 2
        to = ((x + step * (1 - 2 * bit)) * NY + y, gene)
        count = buf.shape[1]
        src[...] = dot3(lows, left(w), NT) + dot3(highs, right(w), NT)
        put(
            src.at[rows((1 - bit) * count, count), :], buf.at[bit],
            send_sem.at[26 + slot], pair_sem.at[slot], to,
        )
        sent(buf.at[0], send_sem.at[26 + slot])
        buf[bit] = src[rows(bit * count, count), :]
        own = w

        def scattering():
            halves(pairself.at[slot, bit], own_gram(own))
            share = pairself.at[slot, bit, :, mine, :]
            put(share, share, send_sem.at[28 + slot], pself_sem.at[slot], to)
            sent(pairself.at[slot, 0, :, pl.ds(0, 128), :], send_sem.at[28 + slot])

        def summing():
            here = early.at[:, rows(order(x, y) * EARLY, EARLY), :]
            here[...] = buf[:, :EARLY, :]
            for d in ALONG_Y:
                put(here, here, send_sem.at[36], earlyx_sem.at[d - 1], at(d, 0, 0))
                put(here, here, send_sem.at[36], earlyy_sem.at[d - 1], at(0, d, 0))
            sent(final.at[pl.ds(0, 30 * EARLY), :], send_sem.at[36])

        def gathering():
            taken(pairself.at[slot, 0, :, pl.ds(0, 128), :], pself_sem.at[slot])
            across = pairself.at[slot, 1 - bit, :, mine, :]
            put(across, across, send_sem.at[30 + slot], pself_sem.at[2 + slot], sibling)
            sent(pairself.at[slot, 0, :, pl.ds(0, 128), :], send_sem.at[30 + slot])
            if level == 3:
                for d in (1, 3, 2):
                    cx, cy = lax.rem(x + NX - d, NX), lax.rem(y + NY - d, NY)
                    taken(early.at[:, pl.ds(0, EARLY), :], earlyx_sem.at[d - 1])
                    first = early.at[0, rows(order(cx, y) * EARLY, EARLY), :]
                    for e in ALONG_Y:
                        put(first, first, send_sem.at[36], early_sem, at(0, e, 0))
                    taken(early.at[:, pl.ds(0, EARLY), :], earlyy_sem.at[d - 1])
                    second = early.at[1, rows(order(x, cy) * EARLY, EARLY), :]
                    for e in ALONG_Y:
                        put(second, second, send_sem.at[36], early_sem, at(e, 0, 0))

        taken(buf.at[0], pair_sem.at[slot])
        lows, highs = split(buf[0]), split(buf[1])
        halves(part.at[level + 1], dot3(lows, highs, TN))
        reduced(level, level + 1, 1, scattering, summing if level == 3 else None, gathering)
        taken(pairself.at[slot, 0, :, pl.ds(0, 128), :], pself_sem.at[2 + slot])
        w = split(
            weights(
                level, joined(pairself[slot, 0]), joined(total[level + 1]), joined(pairself[slot, 1])
            )
        )

    def chunk(cx, cy, skip, count):
        return final.at[pl.ds(pl.multiple_of(order(cx, cy) * PART + EARLY + skip, 8), count), :]

    late = PART - EARLY
    here = chunk(x, y, 0, late)
    here[...] = (dot3(lows, left(w), NT) + dot3(highs, right(w), NT))[EARLY:]
    for d in ALONG_Y:
        put(here, here, send_sem.at[32], finx_sem.at[d - 1], at(d, 0, 0))
        put(here, here, send_sem.at[32], finy_sem.at[d - 1], at(0, d, 0))
    sent(final.at[pl.ds(0, 15 * late), :], send_sem.at[32])

    gram = own_gram(w)
    norm = jnp.sqrt(jnp.sum(gram * gram, keepdims=True) + 1e-06)
    eye = (
        lax.broadcasted_iota(jnp.int32, (ELL, ELL), 0) == lax.broadcasted_iota(jnp.int32, (ELL, ELL), 1)
    ).astype(F32)
    ymat = gram * (1.0 / norm)
    middle = 1.5 * eye - 0.5 * ymat
    zmat = middle
    ymat = dot3(split(ymat), split(middle), NN)

    for d in (1, 3, 2):
        cx, cy = lax.rem(x + NX - d, NX), lax.rem(y + NY - d, NY)
        taken(here, finx_sem.at[d - 1])
        first = chunk(cx, y, 0, 24)
        for e in ALONG_Y:
            put(first, first, send_sem.at[32], fin_sem, at(0, e, 0))
        taken(here, finy_sem.at[d - 1])
        second = chunk(x, cy, 24, late - 24)
        for e in ALONG_Y:
            put(second, second, send_sem.at[32], fin_sem, at(e, 0, 0))

    taken(final.at[pl.ds(0, 18 * EARLY), :], early_sem)
    ahead = dot3(split(early[0]), left(w), NT) + dot3(split(early[1]), right(w), NT)
    for k in range(16):
        final[k * PART:k * PART + EARLY, :] = ahead[k * EARLY:(k + 1) * EARLY]

    def refine(step, carry):
        ymat, zmat = split(carry[0]), split(carry[1])
        middle = split(1.5 * eye - 0.5 * dot3(zmat, ymat, NN))
        return dot3(ymat, middle, NN), dot3(middle, zmat, NN)

    ymat, zmat = lax.fori_loop(0, NS_ITERS - 2, refine, (ymat, zmat))
    ymat, zmat = split(ymat), split(zmat)
    middle = split(1.5 * eye - 0.5 * dot3(zmat, ymat, NN))
    scaled = split(dot3(middle, zmat, NN) * (jnp.sqrt(F32(GENES)) / jnp.sqrt(norm)))

    taken(final.at[pl.ds(0, 9 * late), :], fin_sem)
    hi, lo = split(final[...])
    fh[...] = hi
    fl[...] = lo
    shares = dot2(x_ref[...], (fh[...], fl[...]), NN)
    prod[...] = dot3(scaled, split(shares), NT).reshape(NZ, 2, 16, ELL)

    put(prod.at[:, 1 - c], prodcore, send_sem.at[33], pr_sem.at[0], sibling)
    sent(prodcore, send_sem.at[33])
    taken(prodcore, pr_sem.at[0])
    prodhalf[...] = prod[:, c] + prodcore[...]
    for i in ALONG_Z:
        k = lax.rem(z + i, NZ)
        put(prodhalf.at[k], prodrs.at[i - 1], send_sem.at[34], pr_sem.at[1], (cell, k * 2 + c))
    sent(prodrs, send_sem.at[34])
    basis_ref[...] = dot3(scaled, (fh[...], fl[...]), NT)
    store_basis = pltpu.make_async_copy(basis_ref, basis_hbm, load_sem.at[0])
    store_basis.start()
    taken(prodrs, pr_sem.at[1])
    scores = prodhalf[z]
    for i in range(NZ - 1):
        scores = scores + prodrs[i]
    sq[cell] = jnp.broadcast_to(jnp.sum(scores * scores, axis=1, keepdims=True), (16, 128))
    for dx, dy in PLANES[3]:
        put(sq.at[cell], sq.at[cell], send_sem.at[35], sq_sem, at(dx, dy, 0))
    sent(sq.at[pl.ds(0, 15)], send_sem.at[35])
    taken(sq.at[pl.ds(0, 15)], sq_sem)
    spread = jnp.sum(sq[...], axis=0)[:, :1] * (1.0 / CELLS)
    scores_ref[...] = scores / jnp.sqrt(spread + 1e-05)
    store_basis.wait()
    for like, sem in sends:
        taken(like, sem)


def on_device(expression, mixing):
    vmem = pl.BlockSpec(memory_space=pltpu.VMEM)
    dma = pltpu.SemaphoreType.DMA

    def buf(*shape, kind=F32):
        return pltpu.VMEM(shape, kind)

    basis, scores = pl.pallas_call(
        kernel,
        out_shape=(
            jax.ShapeDtypeStruct((ELL, LOCAL), F32),
            jax.ShapeDtypeStruct((16, ELL), F32),
        ),
        in_specs=[pl.BlockSpec(memory_space=pltpu.HBM)] * 2,
        out_specs=(pl.BlockSpec(memory_space=pltpu.HBM), vmem),
        scratch_shapes=[
            buf(ELL, LOCAL, kind=BF16), buf(4, ELL, 2 * ELL, kind=BF16), buf(ELL, LOCAL),
            buf(LOCAL, ELL), buf(NY, QUART, ELL), buf(5, 2, 256, 128), buf(5, 2, 128, 128),
            buf(5, 2, 128, 128), buf(NYZ - 1, 5, 8, 128), buf(2, 15, 2, 16, 128), buf(2, NZ, 2, 16, 128), buf(5, 2, 256, 128),
            buf(2, 256, 128), buf(2, 128, 128), buf(2, 128, 128), buf(NZ - 1, 2, 16, 128),
            buf(NY, 2, 256, 128),
            buf(QUART, ELL), buf(QUART, ELL), buf(QUART, ELL), buf(2 * PART, ELL),
            buf(2, 2 * PART, ELL), buf(2, PART, ELL), buf(2, 2, 2, 256, 128), buf(2, 16 * EARLY, ELL), buf(LOCAL, ELL),
            buf(2, 2 * ELL, 2 * ELL, kind=BF16), buf(2, 2 * ELL, 2 * ELL, kind=BF16),
            buf(LOCAL, ELL, kind=BF16), buf(LOCAL, ELL, kind=BF16),
            buf(NZ, 2, 16, ELL), buf(NZ, 16, ELL), buf(NZ, 16, ELL), buf(NZ - 1, 16, ELL),
            buf(16, 16, 128),
            dma((2,)), dma((37,)), dma((4,)), dma((4,)), dma((4,)), dma((4,)), dma((2,)),
            dma, dma((5,)), dma((2,)), dma((4,)), dma((3,)), dma((3,)), dma, dma, dma((3,)), dma((3,)), dma((2,)), dma,
        ],
        compiler_params=pltpu.CompilerParams(
            collective_id=0, has_side_effects=True, vmem_limit_bytes=62 * 2**20
        ),
    )(expression, mixing)
    return basis, scores.T


def solution(mesh):
    return jax.shard_map(
        on_device,
        mesh=mesh,
        in_specs=(P("cell", "gene"), P()),
        out_specs=(P(None, "gene"), P("cell", "gene")),
        check_vma=False,
    )
```

```python
import jax
import jax.numpy as jnp
from jax import lax
from jax.experimental import pallas as pl
from jax.experimental.pallas import tpu as pltpu
from jax.sharding import PartitionSpec as P

GENES = 20480
CELLS = 4096
ELL = 256
NS_ITERS = 8
AHEAD = 3
NY, NX, NZ = 4, 4, 8
NYZ = NY * NZ
LOCAL = GENES // 16
QUART = LOCAL // NY
PART = LOCAL // 16
EARLY = PART // 2
MESH = pl.DeviceIdType.MESH
F32 = jnp.float32
BF16 = jnp.bfloat16
NT = (((1,), (1,)), ((), ()))
NN = (((1,), (0,)), ((), ()))
TN = (((0,), (0,)), ((), ()))


def hops(d, n):
    return min(d, n - d)


ALONG_Y = sorted(range(1, NY), key=lambda d: -hops(d, NY))
ALONG_Z = sorted(range(1, NZ), key=lambda d: -hops(d, NZ))
OTHERS = sorted(
    ((dy, dz) for dy in range(NY) for dz in range(NZ) if dy or dz),
    key=lambda d: -hops(d[0], NY) - hops(d[1], NZ),
)
PLANES = {
    2: sorted(
        ((dx, dy) for dx in range(2) for dy in range(NY) if dx or dy),
        key=lambda d: -d[0] - hops(d[1], NY),
    ),
    3: sorted(
        ((dx, dy) for dx in range(NX) for dy in range(NY) if dx or dy),
        key=lambda d: -hops(d[0], NX) - hops(d[1], NY),
    ),
}


def split(a):
    hi = a.astype(BF16)
    return hi, (a - hi.astype(F32)).astype(BF16)


def dot(a, b, dims):
    return lax.dot_general(a, b, dims, preferred_element_type=F32)


def dot2(a, b, dims):
    return dot(a, b[0], dims) + dot(a, b[1], dims)


def dot3(a, b, dims):
    return dot(a[0], b[0], dims) + (dot(a[0], b[1], dims) + dot(a[1], b[0], dims))


def joined(pair):
    return jnp.concatenate([pair[0], pair[1]], axis=1)


def halves(ref, block):
    ref[0] = block[:, :128]
    ref[1] = block[:, 128:]


def kernel(
    x_hbm, mix_hbm, basis_hbm, scores_ref,
    x_ref, mix_ref, basis_ref, xt, rx, part, corebuf, half, rsbuf, cellbuf, zbuf, total,
    selfp, selfcore, selfhalf, selfrs, selfall,
    low, high, quad, mid, pairbuf2, pairbuf3, pairself, early, final,
    gh, gl, fh, fl, prod, prodcore, prodhalf, prodrs, sq,
    load_sem, send_sem, core_sem, rs_sem, ag_sem, cag_sem, z_sem,
    a2a_sem, self_sem, pair_sem, pself_sem, earlyx_sem, earlyy_sem, early_sem, fin_sem, finx_sem, finy_sem, pr_sem, sq_sem,
):
    cell, gene = lax.axis_index("cell"), lax.axis_index("gene")
    x, y = cell // NY, cell % NY
    z, c = gene // 2, gene % 2
    yz = y * NZ + z
    sends = []

    def put(src, dst, send, recv, to):
        copy = pltpu.make_async_remote_copy(
            src_ref=src, dst_ref=dst, send_sem=send, recv_sem=recv,
            device_id=to, device_id_type=MESH,
        )
        copy.start()
        return copy

    def taken(like, sem):
        pltpu.make_async_copy(like, like, sem).wait()

    def sent(like, sem):
        sends.append((like, sem))

    def at(dx, dy, dz):
        return (lax.rem(x + dx, NX) * NY + lax.rem(y + dy, NY), lax.rem(z + dz, NZ) * 2 + c)

    def paired(dx, dy):
        return ((x + dx * (1 - 2 * (x % 2))) * NY + lax.rem(y + dy, NY), gene)

    load_x = pltpu.make_async_copy(x_hbm, x_ref, load_sem.at[0])
    load_mix = pltpu.make_async_copy(mix_hbm, mix_ref, load_sem.at[1])
    load_x.start()
    load_mix.start()
    sibling = (cell, z * 2 + (1 - c))

    barrier = pltpu.get_barrier_semaphore()

    def greet(to):
        pl.semaphore_signal(barrier, inc=1, device_id=to, device_id_type=MESH)

    for d in ALONG_Y:
        greet(at(0, d, 0))
    for d in ALONG_Z:
        greet(at(0, 0, d))
    for d in ALONG_Y:
        greet(at(d, 0, 0))
    greet(sibling)
    load_x.wait()

    for t in range(LOCAL // 128):
        xt[t * 128:(t + 1) * 128, :] = x_ref[:, t * 128:(t + 1) * 128].astype(F32).T
    own = pl.ds(pl.multiple_of(y * QUART, QUART), QUART)
    rx[y] = xt[own, :]
    xb = x_ref[...]
    halves(selfp, dot(xb, xb, NT))
    pl.semaphore_wait(barrier, NZ - 1 + NY - 1 + NX - 1 + 1)

    for i in ALONG_Y:
        q = lax.rem(y + i, NY)
        put(
            xt.at[pl.ds(pl.multiple_of(q * QUART, QUART), QUART), :], rx.at[y],
            send_sem.at[0], a2a_sem, (x * NY + q, gene),
        )
    sent(xt.at[pl.ds(0, 3 * QUART), :], send_sem.at[0])

    def rows(base, count):
        return pl.ds(pl.multiple_of(base, count), count)

    mine = rows(c * 128, 128)
    theirs = rows((1 - c) * 128, 128)

    put(selfp.at[:, theirs, :], selfcore, send_sem.at[1], self_sem.at[0], sibling)
    sent(selfcore, send_sem.at[1])
    taken(selfcore, self_sem.at[0])
    selfhalf[...] = selfp[:, mine, :] + selfcore[...]
    for i in ALONG_Z:
        k = lax.rem(z + i, NZ)
        put(
            selfhalf.at[:, rows(k * 16, 16), :], selfrs.at[i - 1],
            send_sem.at[2], self_sem.at[1], (cell, k * 2 + c),
        )
    sent(selfrs, send_sem.at[2])
    taken(selfrs, self_sem.at[1])
    piece = selfhalf[:, rows(z * 16, 16), :]
    for i in range(NZ - 1):
        piece = piece + selfrs[i]
    place = rows(c * 128 + z * 16, 16)
    selfall[y, :, place, :] = piece
    for i in ALONG_Z:
        k = lax.rem(z + i, NZ)
        put(
            selfall.at[y, :, place, :], selfall.at[y, :, place, :],
            send_sem.at[3], self_sem.at[2], (cell, k * 2 + c),
        )
    sent(selfrs, send_sem.at[3])
    taken(selfrs, self_sem.at[2])
    for i in ALONG_Y:
        q = lax.rem(y + i, NY)
        put(
            selfall.at[y, :, mine, :], selfall.at[y, :, mine, :],
            send_sem.at[4], self_sem.at[3], (x * NY + q, gene),
        )
    sent(selfall.at[pl.ds(0, 3), :, pl.ds(0, 128), :], send_sem.at[4])

    taken(rx.at[pl.ds(0, 3)], a2a_sem)

    def reduced(level, at_block, count, scattering=None, summing=None, gathering=None):
        block = pl.ds(at_block, count)
        sem = 5 + 5 * level
        put(
            part.at[block, :, theirs, :], corebuf.at[block],
            send_sem.at[sem], core_sem.at[level], sibling,
        )
        sent(corebuf.at[block], send_sem.at[sem])
        taken(corebuf.at[block], core_sem.at[level])
        half[block] = part[block, :, mine, :] + corebuf[block]
        if level < 2:
            for dy, dz in OTHERS:
                k = lax.rem(y + dy, NY) * NZ + lax.rem(z + dz, NZ)
                put(
                    half.at[block, k // 16, rows((k % 16) * 8, 8), :],
                    rsbuf.at[dy * NZ + dz - 1, block],
                    send_sem.at[sem + 1], rs_sem.at[level], at(0, dy, dz),
                )
            sent(rsbuf.at[:, block], send_sem.at[sem + 1])
            if scattering is not None:
                scattering()
            taken(rsbuf.at[:, block], rs_sem.at[level])
            tile = half[block, yz // 16, rows((yz % 16) * 8, 8), :]
            for i in range(NYZ - 1):
                tile = tile + rsbuf[i, block]
            piece = total.at[block, yz // 16, rows(c * 128 + (yz % 16) * 8, 8), :]
            piece[...] = tile
            for dy, dz in OTHERS:
                put(piece, piece, send_sem.at[sem + 3], ag_sem.at[level], at(0, dy, dz))
            sent(rsbuf.at[:, block], send_sem.at[sem + 3])
            if gathering is not None:
                gathering()
            taken(rsbuf.at[:, block], ag_sem.at[level])
        else:
            slot = level - 2
            peers = PLANES[level]
            strip = 128 // (len(peers) + 1)
            inbox = cellbuf.at[slot, pl.ds(0, len(peers)), :, pl.ds(0, strip), :]
            whose = (lambda dx, dy: paired(dx, dy)) if level == 2 else (lambda dx, dy: at(dx, dy, 0))
            index = (lambda to: to % 8) if level == 2 else (lambda to: to)
            own = half[at_block, :, rows(index(cell) * strip, strip), :]
            for dx, dy in peers:
                to = whose(dx, dy)
                put(
                    half.at[at_block, :, rows(index(to[0]) * strip, strip), :],
                    cellbuf.at[slot, dx * NY + dy - 1, :, pl.ds(0, strip), :],
                    send_sem.at[sem + 1], rs_sem.at[level], to,
                )
            sent(inbox, send_sem.at[sem + 1])
            taken(inbox, rs_sem.at[level])
            for i in range(len(peers)):
                own = own + cellbuf[slot, i, :, :strip, :]
            share = zbuf.at[slot, z, :, pl.ds(0, strip), :]
            share[...] = own
            for dz in ALONG_Z:
                put(share, share, send_sem.at[sem + 2], z_sem.at[slot], at(0, 0, dz))
            inbox = zbuf.at[slot, pl.ds(0, NZ - 1), :, pl.ds(0, strip), :]
            sent(inbox, send_sem.at[sem + 2])
            if summing is not None:
                summing()
            taken(inbox, z_sem.at[slot])
            own = zbuf[slot, 0, :, :strip, :]
            for i in range(1, NZ):
                own = own + zbuf[slot, i, :, :strip, :]
            piece = total.at[at_block, :, rows(c * 128 + index(cell) * strip, strip), :]
            piece[...] = own
            for dx, dy in peers:
                put(piece, piece, send_sem.at[sem + 3], ag_sem.at[level], whose(dx, dy))
            inbox = cellbuf.at[slot, pl.ds(0, len(peers)), :, pl.ds(0, strip), :]
            sent(inbox, send_sem.at[sem + 3])
            gathering()
            taken(inbox, ag_sem.at[level])
        put(
            total.at[block, :, mine, :], total.at[block, :, mine, :],
            send_sem.at[sem + 4], cag_sem.at[level], sibling,
        )
        sent(corebuf.at[block], send_sem.at[sem + 4])
        taken(corebuf.at[block], cag_sem.at[level])

    def weights(level, lower, cross, upper, slot=0):
        gram = jnp.concatenate(
            [
                jnp.concatenate([lower, cross], axis=1),
                jnp.concatenate([cross.T, upper], axis=1),
            ],
            axis=0,
        )
        inv = 1.0 / jnp.sqrt(jnp.sum(gram * gram, keepdims=True) + 1e-06)
        hi, lo = split(gram)
        gh[slot] = hi
        gl[slot] = lo
        mix = mix_ref[level]
        once = dot2(mix, (gh[slot], gl[slot]), NN)
        twice = dot3(split(once), (gh[slot], gl[slot]), NN)
        return 0.5 * mix.astype(F32) + once * inv - (0.5 * twice) * (inv * inv)

    def own_gram(w, slot=0):
        return dot3(split(dot3(w, (gh[slot], gl[slot]), NN)), w, NT)

    def left(w):
        return w[0][:, :ELL], w[1][:, :ELL]

    def right(w):
        return w[0][:, ELL:], w[1][:, ELL:]

    for p in range(2):
        halves(part.at[p], dot(rx[2 * p].astype(BF16), rx[2 * p + 1].astype(BF16), TN))

    def swap_selves():
        taken(selfall.at[pl.ds(0, 3), :, pl.ds(0, 128), :], self_sem.at[3])
        put(
            selfall.at[:, :, mine, :], selfall.at[:, :, mine, :],
            send_sem.at[25], self_sem.at[4], sibling,
        )
        sent(selfall.at[:, :, pl.ds(0, 128), :], send_sem.at[25])

    reduced(0, 0, 2, gathering=swap_selves)
    load_mix.wait()
    taken(selfall.at[:, :, pl.ds(0, 128), :], self_sem.at[4])
    kept = []
    for p, sketch in ((0, low), (1, high)):
        w = split(weights(0, joined(selfall[2 * p]), joined(total[p]), joined(selfall[2 * p + 1]), p))
        sketch[...] = dot2(rx[2 * p].astype(BF16), left(w), NT) + dot2(
            rx[2 * p + 1].astype(BF16), right(w), NT
        )
        kept.append(w)

    lows, highs = split(low[...]), split(high[...])
    halves(part.at[2], dot3(lows, highs, TN))
    grams = []
    reduced(1, 2, 1, lambda: grams.extend(own_gram(kept[p], p) for p in range(2)))
    w = split(weights(1, grams[0], joined(total[2]), grams[1]))

    def order(cx, cy):
        return cy * 4 + cx % 2 * 2 + cx // 2

    for level, step, src, buf in ((2, 1, quad, pairbuf2), (3, 2, mid, pairbuf3)):
        slot = level - 2
        bit = x // step % 2
        to = ((x + step * (1 - 2 * bit)) * NY + y, gene)
        count = buf.shape[1]
        src[...] = dot3(lows, left(w), NT) + dot3(highs, right(w), NT)
        put(
            src.at[rows((1 - bit) * count, count), :], buf.at[bit],
            send_sem.at[26 + slot], pair_sem.at[slot], to,
        )
        sent(buf.at[0], send_sem.at[26 + slot])
        buf[bit] = src[rows(bit * count, count), :]
        halves(pairself.at[slot, bit], own_gram(w))
        share = pairself.at[slot, bit, :, mine, :]
        put(share, share, send_sem.at[28 + slot], pself_sem.at[slot], to)
        sent(pairself.at[slot, 0, :, pl.ds(0, 128), :], send_sem.at[28 + slot])

        def summing():
            here = early.at[:, rows(order(x, y) * EARLY, EARLY), :]
            here[...] = buf[:, :EARLY, :]
            for d in ALONG_Y:
                put(here, here, send_sem.at[36], earlyx_sem.at[d - 1], at(d, 0, 0))
                put(here, here, send_sem.at[36], earlyy_sem.at[d - 1], at(0, d, 0))
            sent(final.at[pl.ds(0, 30 * EARLY), :], send_sem.at[36])

        def gathering():
            taken(pairself.at[slot, 0, :, pl.ds(0, 128), :], pself_sem.at[slot])
            across = pairself.at[slot, 1 - bit, :, mine, :]
            put(across, across, send_sem.at[30 + slot], pself_sem.at[2 + slot], sibling)
            sent(pairself.at[slot, 0, :, pl.ds(0, 128), :], send_sem.at[30 + slot])
            if level == 3:
                for d in (1, 3, 2):
                    cx, cy = lax.rem(x + NX - d, NX), lax.rem(y + NY - d, NY)
                    taken(early.at[:, pl.ds(0, EARLY), :], earlyx_sem.at[d - 1])
                    first = early.at[0, rows(order(cx, y) * EARLY, EARLY), :]
                    for e in ALONG_Y:
                        put(first, first, send_sem.at[36], early_sem, at(0, e, 0))
                    taken(early.at[:, pl.ds(0, EARLY), :], earlyy_sem.at[d - 1])
                    second = early.at[1, rows(order(x, cy) * EARLY, EARLY), :]
                    for e in ALONG_Y:
                        put(second, second, send_sem.at[36], early_sem, at(e, 0, 0))

        taken(buf.at[0], pair_sem.at[slot])
        lows, highs = split(buf[0]), split(buf[1])
        halves(part.at[level + 1], dot3(lows, highs, TN))
        reduced(level, level + 1, 1, None, summing if level == 3 else None, gathering)
        taken(pairself.at[slot, 0, :, pl.ds(0, 128), :], pself_sem.at[2 + slot])
        w = split(
            weights(
                level, joined(pairself[slot, 0]), joined(total[level + 1]), joined(pairself[slot, 1])
            )
        )

    def chunk(cx, cy, skip, count):
        return final.at[pl.ds(pl.multiple_of(order(cx, cy) * PART + EARLY + skip, 8), count), :]

    late = PART - EARLY
    here = chunk(x, y, 0, late)
    here[...] = (dot3(lows, left(w), NT) + dot3(highs, right(w), NT))[EARLY:]
    for d in ALONG_Y:
        put(here, here, send_sem.at[32], finx_sem.at[d - 1], at(d, 0, 0))
        put(here, here, send_sem.at[32], finy_sem.at[d - 1], at(0, d, 0))
    sent(final.at[pl.ds(0, 15 * late), :], send_sem.at[32])

    gram = own_gram(w)
    norm = jnp.sqrt(jnp.sum(gram * gram, keepdims=True) + 1e-06)
    eye = (
        lax.broadcasted_iota(jnp.int32, (ELL, ELL), 0) == lax.broadcasted_iota(jnp.int32, (ELL, ELL), 1)
    ).astype(F32)
    ymat = gram * (1.0 / norm)
    middle = 1.5 * eye - 0.5 * ymat
    zmat = middle
    ymat = dot3(split(ymat), split(middle), NN)

    def refine(step, carry):
        ymat, zmat = split(carry[0]), split(carry[1])
        middle = split(1.5 * eye - 0.5 * dot3(zmat, ymat, NN))
        return dot3(ymat, middle, NN), dot3(middle, zmat, NN)

    ymat, zmat = lax.fori_loop(0, AHEAD, refine, (ymat, zmat))

    for d in (1, 3, 2):
        cx, cy = lax.rem(x + NX - d, NX), lax.rem(y + NY - d, NY)
        taken(here, finx_sem.at[d - 1])
        first = chunk(cx, y, 0, 24)
        for e in ALONG_Y:
            put(first, first, send_sem.at[32], fin_sem, at(0, e, 0))
        taken(here, finy_sem.at[d - 1])
        second = chunk(x, cy, 24, late - 24)
        for e in ALONG_Y:
            put(second, second, send_sem.at[32], fin_sem, at(e, 0, 0))

    taken(final.at[pl.ds(0, 18 * EARLY), :], early_sem)
    ahead = dot3(split(early[0]), left(w), NT) + dot3(split(early[1]), right(w), NT)
    for k in range(16):
        final[k * PART:k * PART + EARLY, :] = ahead[k * EARLY:(k + 1) * EARLY]

    ymat, zmat = lax.fori_loop(AHEAD, NS_ITERS - 2, refine, (ymat, zmat))
    ymat, zmat = split(ymat), split(zmat)
    middle = split(1.5 * eye - 0.5 * dot3(zmat, ymat, NN))
    scaled = split(dot3(middle, zmat, NN) * (jnp.sqrt(F32(GENES)) / jnp.sqrt(norm)))

    taken(final.at[pl.ds(0, 9 * late), :], fin_sem)
    hi, lo = split(final[...])
    fh[...] = hi
    fl[...] = lo
    shares = dot2(x_ref[...], (fh[...], fl[...]), NN)
    prod[...] = dot3(scaled, split(shares), NT).reshape(NZ, 2, 16, ELL)

    put(prod.at[:, 1 - c], prodcore, send_sem.at[33], pr_sem.at[0], sibling)
    sent(prodcore, send_sem.at[33])
    taken(prodcore, pr_sem.at[0])
    prodhalf[...] = prod[:, c] + prodcore[...]
    for i in ALONG_Z:
        k = lax.rem(z + i, NZ)
        put(prodhalf.at[k], prodrs.at[i - 1], send_sem.at[34], pr_sem.at[1], (cell, k * 2 + c))
    sent(prodrs, send_sem.at[34])
    basis_ref[...] = dot3(scaled, (fh[...], fl[...]), NT)
    store_basis = pltpu.make_async_copy(basis_ref, basis_hbm, load_sem.at[0])
    store_basis.start()
    taken(prodrs, pr_sem.at[1])
    scores = prodhalf[z]
    for i in range(NZ - 1):
        scores = scores + prodrs[i]
    sq[cell] = jnp.broadcast_to(jnp.sum(scores * scores, axis=1, keepdims=True), (16, 128))
    for dx, dy in PLANES[3]:
        put(sq.at[cell], sq.at[cell], send_sem.at[35], sq_sem, at(dx, dy, 0))
    sent(sq.at[pl.ds(0, 15)], send_sem.at[35])
    taken(sq.at[pl.ds(0, 15)], sq_sem)
    spread = jnp.sum(sq[...], axis=0)[:, :1] * (1.0 / CELLS)
    scores_ref[...] = scores / jnp.sqrt(spread + 1e-05)
    store_basis.wait()
    for like, sem in sends:
        taken(like, sem)


def on_device(expression, mixing):
    vmem = pl.BlockSpec(memory_space=pltpu.VMEM)
    dma = pltpu.SemaphoreType.DMA

    def buf(*shape, kind=F32):
        return pltpu.VMEM(shape, kind)

    basis, scores = pl.pallas_call(
        kernel,
        out_shape=(
            jax.ShapeDtypeStruct((ELL, LOCAL), F32),
            jax.ShapeDtypeStruct((16, ELL), F32),
        ),
        in_specs=[pl.BlockSpec(memory_space=pltpu.HBM)] * 2,
        out_specs=(pl.BlockSpec(memory_space=pltpu.HBM), vmem),
        scratch_shapes=[
            buf(ELL, LOCAL, kind=BF16), buf(4, ELL, 2 * ELL, kind=BF16), buf(ELL, LOCAL),
            buf(LOCAL, ELL), buf(NY, QUART, ELL), buf(5, 2, 256, 128), buf(5, 2, 128, 128),
            buf(5, 2, 128, 128), buf(NYZ - 1, 5, 8, 128), buf(2, 15, 2, 16, 128), buf(2, NZ, 2, 16, 128), buf(5, 2, 256, 128),
            buf(2, 256, 128), buf(2, 128, 128), buf(2, 128, 128), buf(NZ - 1, 2, 16, 128),
            buf(NY, 2, 256, 128),
            buf(QUART, ELL), buf(QUART, ELL), buf(QUART, ELL), buf(2 * PART, ELL),
            buf(2, 2 * PART, ELL), buf(2, PART, ELL), buf(2, 2, 2, 256, 128), buf(2, 16 * EARLY, ELL), buf(LOCAL, ELL),
            buf(2, 2 * ELL, 2 * ELL, kind=BF16), buf(2, 2 * ELL, 2 * ELL, kind=BF16),
            buf(LOCAL, ELL, kind=BF16), buf(LOCAL, ELL, kind=BF16),
            buf(NZ, 2, 16, ELL), buf(NZ, 16, ELL), buf(NZ, 16, ELL), buf(NZ - 1, 16, ELL),
            buf(16, 16, 128),
            dma((2,)), dma((37,)), dma((4,)), dma((4,)), dma((4,)), dma((4,)), dma((2,)),
            dma, dma((5,)), dma((2,)), dma((4,)), dma((3,)), dma((3,)), dma, dma, dma((3,)), dma((3,)), dma((2,)), dma,
        ],
        compiler_params=pltpu.CompilerParams(
            collective_id=0, has_side_effects=True, vmem_limit_bytes=62 * 2**20
        ),
    )(expression, mixing)
    return basis, scores.T


def solution(mesh):
    return jax.shard_map(
        on_device,
        mesh=mesh,
        in_specs=(P("cell", "gene"), P()),
        out_specs=(P(None, "gene"), P("cell", "gene")),
        check_vma=False,
    )
```

```python
import jax
import jax.numpy as jnp
from jax import lax
from jax.experimental import pallas as pl
from jax.experimental.pallas import tpu as pltpu
from jax.sharding import PartitionSpec as P

GENES = 20480
CELLS = 4096
ELL = 256
NS_ITERS = 8
AHEAD = 3
NY, NX, NZ = 4, 4, 8
NYZ = NY * NZ
LOCAL = GENES // 16
QUART = LOCAL // NY
PART = LOCAL // 16
EARLY = PART // 2
MESH = pl.DeviceIdType.MESH
F32 = jnp.float32
BF16 = jnp.bfloat16
NT = (((1,), (1,)), ((), ()))
NN = (((1,), (0,)), ((), ()))
TN = (((0,), (0,)), ((), ()))


def hops(d, n):
    return min(d, n - d)


ALONG_Y = sorted(range(1, NY), key=lambda d: -hops(d, NY))
ALONG_Z = sorted(range(1, NZ), key=lambda d: -hops(d, NZ))
OTHERS = sorted(
    ((dy, dz) for dy in range(NY) for dz in range(NZ) if dy or dz),
    key=lambda d: -hops(d[0], NY) - hops(d[1], NZ),
)
PLANES = {
    2: sorted(
        ((dx, dy) for dx in range(2) for dy in range(NY) if dx or dy),
        key=lambda d: -d[0] - hops(d[1], NY),
    ),
    3: sorted(
        ((dx, dy) for dx in range(NX) for dy in range(NY) if dx or dy),
        key=lambda d: -hops(d[0], NX) - hops(d[1], NY),
    ),
}


def split(a):
    hi = a.astype(BF16)
    return hi, (a - hi.astype(F32)).astype(BF16)


def dot(a, b, dims):
    return lax.dot_general(a, b, dims, preferred_element_type=F32)


def dot2(a, b, dims):
    return dot(a, b[0], dims) + dot(a, b[1], dims)


def dot3(a, b, dims):
    return dot(a[0], b[0], dims) + (dot(a[0], b[1], dims) + dot(a[1], b[0], dims))


def joined(pair):
    return jnp.concatenate([pair[0], pair[1]], axis=1)


def halves(ref, block):
    ref[0] = block[:, :128]
    ref[1] = block[:, 128:]


def kernel(
    x_hbm, mix_hbm, basis_hbm, scores_ref,
    x_ref, mix_ref, basis_ref, xt, rx, part, corebuf, half, rsbuf, cellbuf, zbuf, total,
    selfp, selfcore, selfhalf, selfrs, selfall,
    low, high, quad, mid, pairbuf2, pairbuf3, pairself, early, final,
    stash, gh, gl, fh, fl, prod, prodcore, prodhalf, prodrs, sq,
    load_sem, send_sem, core_sem, rs_sem, ag_sem, cag_sem, z_sem,
    a2a_sem, self_sem, pair_sem, pself_sem, earlyx_sem, earlyy_sem, early_sem, fin_sem, finx_sem, finy_sem, pr_sem, sq_sem,
):
    cell, gene = lax.axis_index("cell"), lax.axis_index("gene")
    x, y = cell // NY, cell % NY
    z, c = gene // 2, gene % 2
    yz = y * NZ + z
    sends = []

    def put(src, dst, send, recv, to):
        copy = pltpu.make_async_remote_copy(
            src_ref=src, dst_ref=dst, send_sem=send, recv_sem=recv,
            device_id=to, device_id_type=MESH,
        )
        copy.start()
        return copy

    def taken(like, sem):
        pltpu.make_async_copy(like, like, sem).wait()

    def sent(like, sem):
        sends.append((like, sem))

    def at(dx, dy, dz):
        return (lax.rem(x + dx, NX) * NY + lax.rem(y + dy, NY), lax.rem(z + dz, NZ) * 2 + c)

    def paired(dx, dy):
        return ((x + dx * (1 - 2 * (x % 2))) * NY + lax.rem(y + dy, NY), gene)

    load_x = pltpu.make_async_copy(x_hbm, x_ref, load_sem.at[0])
    load_mix = pltpu.make_async_copy(mix_hbm, mix_ref, load_sem.at[1])
    load_x.start()
    load_mix.start()
    sibling = (cell, z * 2 + (1 - c))

    barrier = pltpu.get_barrier_semaphore()

    def greet(to):
        pl.semaphore_signal(barrier, inc=1, device_id=to, device_id_type=MESH)

    for d in ALONG_Y:
        greet(at(0, d, 0))
    for d in ALONG_Z:
        greet(at(0, 0, d))
    for d in ALONG_Y:
        greet(at(d, 0, 0))
    greet(sibling)
    load_x.wait()

    for t in range(LOCAL // 128):
        xt[t * 128:(t + 1) * 128, :] = x_ref[:, t * 128:(t + 1) * 128].astype(F32).T
    own = pl.ds(pl.multiple_of(y * QUART, QUART), QUART)
    rx[y] = xt[own, :]
    xb = x_ref[...]
    halves(selfp, dot(xb, xb, NT))
    pl.semaphore_wait(barrier, NZ - 1 + NY - 1 + NX - 1 + 1)

    for i in ALONG_Y:
        q = lax.rem(y + i, NY)
        put(
            xt.at[pl.ds(pl.multiple_of(q * QUART, QUART), QUART), :], rx.at[y],
            send_sem.at[0], a2a_sem, (x * NY + q, gene),
        )
    sent(xt.at[pl.ds(0, 3 * QUART), :], send_sem.at[0])

    def rows(base, count):
        return pl.ds(pl.multiple_of(base, count), count)

    mine = rows(c * 128, 128)
    theirs = rows((1 - c) * 128, 128)

    put(selfp.at[:, theirs, :], selfcore, send_sem.at[1], self_sem.at[0], sibling)
    sent(selfcore, send_sem.at[1])
    taken(selfcore, self_sem.at[0])
    selfhalf[...] = selfp[:, mine, :] + selfcore[...]
    for i in ALONG_Z:
        k = lax.rem(z + i, NZ)
        put(
            selfhalf.at[:, rows(k * 16, 16), :], selfrs.at[i - 1],
            send_sem.at[2], self_sem.at[1], (cell, k * 2 + c),
        )
    sent(selfrs, send_sem.at[2])
    taken(selfrs, self_sem.at[1])
    piece = selfhalf[:, rows(z * 16, 16), :]
    for i in range(NZ - 1):
        piece = piece + selfrs[i]
    place = rows(c * 128 + z * 16, 16)
    selfall[y, :, place, :] = piece
    for i in ALONG_Z:
        k = lax.rem(z + i, NZ)
        put(
            selfall.at[y, :, place, :], selfall.at[y, :, place, :],
            send_sem.at[3], self_sem.at[2], (cell, k * 2 + c),
        )
    sent(selfrs, send_sem.at[3])
    taken(selfrs, self_sem.at[2])
    for i in ALONG_Y:
        q = lax.rem(y + i, NY)
        put(
            selfall.at[y, :, mine, :], selfall.at[y, :, mine, :],
            send_sem.at[4], self_sem.at[3], (x * NY + q, gene),
        )
    sent(selfall.at[pl.ds(0, 3), :, pl.ds(0, 128), :], send_sem.at[4])

    taken(rx.at[pl.ds(0, 3)], a2a_sem)

    def reduced(level, at_block, count, cross, scattering=None, summing=None, gathering=None):
        block = pl.ds(at_block, count)
        sem = 5 + 5 * level
        cross(1 - c)
        put(
            part.at[block, :, theirs, :], corebuf.at[block],
            send_sem.at[sem], core_sem.at[level], sibling,
        )
        sent(corebuf.at[block], send_sem.at[sem])
        cross(c)
        taken(corebuf.at[block], core_sem.at[level])
        half[block] = part[block, :, mine, :] + corebuf[block]
        if level < 2:
            for dy, dz in OTHERS:
                k = lax.rem(y + dy, NY) * NZ + lax.rem(z + dz, NZ)
                put(
                    half.at[block, k // 16, rows((k % 16) * 8, 8), :],
                    rsbuf.at[dy * NZ + dz - 1, block],
                    send_sem.at[sem + 1], rs_sem.at[level], at(0, dy, dz),
                )
            sent(rsbuf.at[:, block], send_sem.at[sem + 1])
            if scattering is not None:
                scattering()
            taken(rsbuf.at[:, block], rs_sem.at[level])
            tile = half[block, yz // 16, rows((yz % 16) * 8, 8), :]
            for i in range(NYZ - 1):
                tile = tile + rsbuf[i, block]
            piece = total.at[block, yz // 16, rows(c * 128 + (yz % 16) * 8, 8), :]
            piece[...] = tile
            for dy, dz in OTHERS:
                put(piece, piece, send_sem.at[sem + 3], ag_sem.at[level], at(0, dy, dz))
            sent(rsbuf.at[:, block], send_sem.at[sem + 3])
            if gathering is not None:
                gathering()
            taken(rsbuf.at[:, block], ag_sem.at[level])
        else:
            slot = level - 2
            peers = PLANES[level]
            strip = 128 // (len(peers) + 1)
            inbox = cellbuf.at[slot, pl.ds(0, len(peers)), :, pl.ds(0, strip), :]
            whose = (lambda dx, dy: paired(dx, dy)) if level == 2 else (lambda dx, dy: at(dx, dy, 0))
            index = (lambda to: to % 8) if level == 2 else (lambda to: to)
            own = half[at_block, :, rows(index(cell) * strip, strip), :]
            for dx, dy in peers:
                to = whose(dx, dy)
                put(
                    half.at[at_block, :, rows(index(to[0]) * strip, strip), :],
                    cellbuf.at[slot, dx * NY + dy - 1, :, pl.ds(0, strip), :],
                    send_sem.at[sem + 1], rs_sem.at[level], to,
                )
            sent(inbox, send_sem.at[sem + 1])
            taken(inbox, rs_sem.at[level])
            for i in range(len(peers)):
                own = own + cellbuf[slot, i, :, :strip, :]
            share = zbuf.at[slot, z, :, pl.ds(0, strip), :]
            share[...] = own
            for dz in ALONG_Z:
                put(share, share, send_sem.at[sem + 2], z_sem.at[slot], at(0, 0, dz))
            inbox = zbuf.at[slot, pl.ds(0, NZ - 1), :, pl.ds(0, strip), :]
            sent(inbox, send_sem.at[sem + 2])
            if summing is not None:
                summing()
            taken(inbox, z_sem.at[slot])
            own = zbuf[slot, 0, :, :strip, :]
            for i in range(1, NZ):
                own = own + zbuf[slot, i, :, :strip, :]
            piece = total.at[at_block, :, rows(c * 128 + index(cell) * strip, strip), :]
            piece[...] = own
            for dx, dy in peers:
                put(piece, piece, send_sem.at[sem + 3], ag_sem.at[level], whose(dx, dy))
            inbox = cellbuf.at[slot, pl.ds(0, len(peers)), :, pl.ds(0, strip), :]
            sent(inbox, send_sem.at[sem + 3])
            gathering()
            taken(inbox, ag_sem.at[level])
        put(
            total.at[block, :, mine, :], total.at[block, :, mine, :],
            send_sem.at[sem + 4], cag_sem.at[level], sibling,
        )
        sent(corebuf.at[block], send_sem.at[sem + 4])
        taken(corebuf.at[block], cag_sem.at[level])

    def prepare(level, lower, upper, slot=0):
        for at_row, gram in ((0, lower), (ELL, upper)):
            spot = slice(at_row, at_row + ELL)
            gh[slot, spot, spot], gl[slot, spot, spot] = split(gram)
        mix = mix_ref[level]
        first = dot2(mix[:, :ELL], (gh[slot, :ELL, :ELL], gl[slot, :ELL, :ELL]), NN)
        second = dot2(mix[:, ELL:], (gh[slot, ELL:, ELL:], gl[slot, ELL:, ELL:]), NN)
        squares = jnp.sum(lower * lower, keepdims=True) + jnp.sum(upper * upper, keepdims=True)
        return first, second, squares

    def weights(level, cross, ready, slot=0):
        first, second, squares = ready
        inv = 1.0 / jnp.sqrt(squares + 2.0 * jnp.sum(cross * cross, keepdims=True) + 1e-06)
        over, under = split(cross), split(cross.T)
        gh[slot, :ELL, ELL:], gl[slot, :ELL, ELL:] = over
        gh[slot, ELL:, :ELL], gl[slot, ELL:, :ELL] = under
        mix = mix_ref[level]
        once = jnp.concatenate(
            [first + dot2(mix[:, ELL:], under, NN), second + dot2(mix[:, :ELL], over, NN)], axis=1
        )
        twice = dot3(split(once), (gh[slot], gl[slot]), NN)
        return 0.5 * mix.astype(F32) + once * inv - (0.5 * twice) * (inv * inv)

    def own_gram(w, slot=0):
        return dot3(split(dot3(w, (gh[slot], gl[slot]), NN)), w, NT)

    def left(w):
        return w[0][:, :ELL], w[1][:, :ELL]

    def right(w):
        return w[0][:, ELL:], w[1][:, ELL:]

    def stashed(base, count):
        at_rows = rows(base, count) if base is not None else pl.ds(0, count)
        return (stash[0, at_rows, :], stash[1, at_rows, :]), (stash[2, at_rows, :], stash[3, at_rows, :])

    def sketched(w, base, count):
        lower, upper = stashed(base, count)
        return dot3(lower, left(w), NT) + dot3(upper, right(w), NT)

    def crossed(at_block, count):
        def cross(side):
            side_rows = rows(side * 128, 128)
            lower = stash[0, :count, side_rows], stash[1, :count, side_rows]
            block = dot3(lower, stashed(None, count)[1], TN)
            part[at_block, 0, side_rows, :] = block[:, :128]
            part[at_block, 1, side_rows, :] = block[:, 128:]

        return cross

    def keep(lower, upper):
        count = lower.shape[0]
        stash[0, :count], stash[1, :count] = split(lower)
        stash[2, :count], stash[3, :count] = split(upper)

    for i in range(NY):
        stash[i] = rx[i].astype(BF16)

    def cross_batches(side):
        side_rows = rows(side * 128, 128)
        for p in range(2):
            block = dot(stash[2 * p, :, side_rows], stash[2 * p + 1], TN)
            part[p, 0, side_rows, :] = block[:, :128]
            part[p, 1, side_rows, :] = block[:, 128:]

    ready = []

    def swap_selves():
        taken(selfall.at[pl.ds(0, 3), :, pl.ds(0, 128), :], self_sem.at[3])
        put(
            selfall.at[:, :, mine, :], selfall.at[:, :, mine, :],
            send_sem.at[25], self_sem.at[4], sibling,
        )
        sent(selfall.at[:, :, pl.ds(0, 128), :], send_sem.at[25])
        load_mix.wait()
        taken(selfall.at[:, :, pl.ds(0, 128), :], self_sem.at[4])
        for p in range(2):
            ready.append(prepare(0, joined(selfall[2 * p]), joined(selfall[2 * p + 1]), p))

    reduced(0, 0, 2, cross_batches, gathering=swap_selves)
    kept = []
    for p, sketch in ((0, low), (1, high)):
        w = split(weights(0, joined(total[p]), ready[p], p))
        sketch[...] = dot2(stash[2 * p], left(w), NT) + dot2(stash[2 * p + 1], right(w), NT)
        kept.append(w)

    keep(low[...], high[...])
    grams = []
    reduced(
        1, 2, 1, crossed(2, QUART),
        scattering=lambda: grams.extend(own_gram(kept[p], p) for p in range(2)),
        gathering=lambda: ready.append(prepare(1, *grams)),
    )
    w = split(weights(1, joined(total[2]), ready[-1]))

    def order(cx, cy):
        return cy * 4 + cx % 2 * 2 + cx // 2

    for level, step, src, buf in ((2, 1, quad, pairbuf2), (3, 2, mid, pairbuf3)):
        slot = level - 2
        bit = x // step % 2
        to = ((x + step * (1 - 2 * bit)) * NY + y, gene)
        count = buf.shape[1]
        src[...] = sketched(w, (1 - bit) * count, count)
        put(src, buf.at[bit], send_sem.at[26 + slot], pair_sem.at[slot], to)
        sent(buf.at[0], send_sem.at[26 + slot])
        buf[bit] = sketched(w, bit * count, count)
        halves(pairself.at[slot, bit], own_gram(w))
        share = pairself.at[slot, bit, :, mine, :]
        put(share, share, send_sem.at[28 + slot], pself_sem.at[slot], to)
        sent(pairself.at[slot, 0, :, pl.ds(0, 128), :], send_sem.at[28 + slot])

        def summing():
            here = early.at[:, rows(order(x, y) * EARLY, EARLY), :]
            here[...] = buf[:, :EARLY, :]
            for d in ALONG_Y:
                put(here, here, send_sem.at[36], earlyx_sem.at[d - 1], at(d, 0, 0))
                put(here, here, send_sem.at[36], earlyy_sem.at[d - 1], at(0, d, 0))
            sent(final.at[pl.ds(0, 30 * EARLY), :], send_sem.at[36])

        def gathering():
            taken(pairself.at[slot, 0, :, pl.ds(0, 128), :], pself_sem.at[slot])
            across = pairself.at[slot, 1 - bit, :, mine, :]
            put(across, across, send_sem.at[30 + slot], pself_sem.at[2 + slot], sibling)
            sent(pairself.at[slot, 0, :, pl.ds(0, 128), :], send_sem.at[30 + slot])
            if level == 3:
                for d in (1, 3, 2):
                    cx, cy = lax.rem(x + NX - d, NX), lax.rem(y + NY - d, NY)
                    taken(early.at[:, pl.ds(0, EARLY), :], earlyx_sem.at[d - 1])
                    first = early.at[0, rows(order(cx, y) * EARLY, EARLY), :]
                    for e in ALONG_Y:
                        put(first, first, send_sem.at[36], early_sem, at(0, e, 0))
                    taken(early.at[:, pl.ds(0, EARLY), :], earlyy_sem.at[d - 1])
                    second = early.at[1, rows(order(x, cy) * EARLY, EARLY), :]
                    for e in ALONG_Y:
                        put(second, second, send_sem.at[36], early_sem, at(e, 0, 0))
            taken(pairself.at[slot, 0, :, pl.ds(0, 128), :], pself_sem.at[2 + slot])
            ready.append(prepare(level, joined(pairself[slot, 0]), joined(pairself[slot, 1])))

        taken(buf.at[0], pair_sem.at[slot])
        keep(buf[0], buf[1])
        reduced(
            level, level + 1, 1, crossed(level + 1, count),
            summing=summing if level == 3 else None, gathering=gathering,
        )
        w = split(weights(level, joined(total[level + 1]), ready[-1]))

    def chunk(cx, cy, skip, count):
        return final.at[pl.ds(pl.multiple_of(order(cx, cy) * PART + EARLY + skip, 8), count), :]

    late = PART - EARLY
    here = chunk(x, y, 0, late)
    here[...] = sketched(w, None, PART)[EARLY:]
    for d in ALONG_Y:
        put(here, here, send_sem.at[32], finx_sem.at[d - 1], at(d, 0, 0))
        put(here, here, send_sem.at[32], finy_sem.at[d - 1], at(0, d, 0))
    sent(final.at[pl.ds(0, 15 * late), :], send_sem.at[32])

    gram = own_gram(w)
    norm = jnp.sqrt(jnp.sum(gram * gram, keepdims=True) + 1e-06)
    eye = (
        lax.broadcasted_iota(jnp.int32, (ELL, ELL), 0) == lax.broadcasted_iota(jnp.int32, (ELL, ELL), 1)
    ).astype(F32)
    ymat = gram * (1.0 / norm)
    middle = 1.5 * eye - 0.5 * ymat
    zmat = middle
    ymat = dot3(split(ymat), split(middle), NN)

    def refine(step, carry):
        ymat, zmat = split(carry[0]), split(carry[1])
        middle = split(1.5 * eye - 0.5 * dot3(zmat, ymat, NN))
        return dot3(ymat, middle, NN), dot3(middle, zmat, NN)

    ymat, zmat = lax.fori_loop(0, AHEAD, refine, (ymat, zmat))

    for d in (1, 3, 2):
        cx, cy = lax.rem(x + NX - d, NX), lax.rem(y + NY - d, NY)
        taken(here, finx_sem.at[d - 1])
        first = chunk(cx, y, 0, 24)
        for e in ALONG_Y:
            put(first, first, send_sem.at[32], fin_sem, at(0, e, 0))
        taken(here, finy_sem.at[d - 1])
        second = chunk(x, cy, 24, late - 24)
        for e in ALONG_Y:
            put(second, second, send_sem.at[32], fin_sem, at(e, 0, 0))

    taken(final.at[pl.ds(0, 18 * EARLY), :], early_sem)
    ahead = dot3(split(early[0]), left(w), NT) + dot3(split(early[1]), right(w), NT)
    for k in range(16):
        final[k * PART:k * PART + EARLY, :] = ahead[k * EARLY:(k + 1) * EARLY]

    ymat, zmat = lax.fori_loop(AHEAD, NS_ITERS - 2, refine, (ymat, zmat))
    ymat, zmat = split(ymat), split(zmat)
    middle = split(1.5 * eye - 0.5 * dot3(zmat, ymat, NN))
    scaled = split(dot3(middle, zmat, NN) * (jnp.sqrt(F32(GENES)) / jnp.sqrt(norm)))

    taken(final.at[pl.ds(0, 9 * late), :], fin_sem)
    hi, lo = split(final[...])
    fh[...] = hi
    fl[...] = lo
    shares = dot2(x_ref[...], (fh[...], fl[...]), NN)
    prod[...] = dot3(scaled, split(shares), NT).reshape(NZ, 2, 16, ELL)

    put(prod.at[:, 1 - c], prodcore, send_sem.at[33], pr_sem.at[0], sibling)
    sent(prodcore, send_sem.at[33])
    taken(prodcore, pr_sem.at[0])
    prodhalf[...] = prod[:, c] + prodcore[...]
    for i in ALONG_Z:
        k = lax.rem(z + i, NZ)
        put(prodhalf.at[k], prodrs.at[i - 1], send_sem.at[34], pr_sem.at[1], (cell, k * 2 + c))
    sent(prodrs, send_sem.at[34])
    basis_ref[...] = dot3(scaled, (fh[...], fl[...]), NT)
    store_basis = pltpu.make_async_copy(basis_ref, basis_hbm, load_sem.at[0])
    store_basis.start()
    taken(prodrs, pr_sem.at[1])
    scores = prodhalf[z]
    for i in range(NZ - 1):
        scores = scores + prodrs[i]
    squares = jnp.sum(scores * scores, axis=1, keepdims=True)
    lane = lax.broadcasted_iota(jnp.int32, (8, 128), 1)
    sq[cell] = jnp.where(
        lane < 64, jnp.broadcast_to(squares[:8], (8, 128)), jnp.broadcast_to(squares[8:], (8, 128))
    )
    for dx, dy in PLANES[3]:
        put(sq.at[cell], sq.at[cell], send_sem.at[35], sq_sem, at(dx, dy, 0))
    sent(sq.at[pl.ds(0, 15)], send_sem.at[35])
    taken(sq.at[pl.ds(0, 15)], sq_sem)
    squares = jnp.sum(sq[...], axis=0)
    spread = jnp.concatenate([squares[:, :1], squares[:, 64:65]], axis=0) * (1.0 / CELLS)
    scores_ref[...] = scores / jnp.sqrt(spread + 1e-05)
    store_basis.wait()
    for like, sem in sends:
        taken(like, sem)


def on_device(expression, mixing):
    vmem = pl.BlockSpec(memory_space=pltpu.VMEM)
    dma = pltpu.SemaphoreType.DMA

    def buf(*shape, kind=F32):
        return pltpu.VMEM(shape, kind)

    basis, scores = pl.pallas_call(
        kernel,
        out_shape=(
            jax.ShapeDtypeStruct((ELL, LOCAL), F32),
            jax.ShapeDtypeStruct((16, ELL), F32),
        ),
        in_specs=[pl.BlockSpec(memory_space=pltpu.HBM)] * 2,
        out_specs=(pl.BlockSpec(memory_space=pltpu.HBM), vmem),
        scratch_shapes=[
            buf(ELL, LOCAL, kind=BF16), buf(4, ELL, 2 * ELL, kind=BF16), buf(ELL, LOCAL),
            buf(LOCAL, ELL), buf(NY, QUART, ELL), buf(5, 2, 256, 128), buf(5, 2, 128, 128),
            buf(5, 2, 128, 128), buf(NYZ - 1, 5, 8, 128), buf(2, 15, 2, 16, 128), buf(2, NZ, 2, 16, 128), buf(5, 2, 256, 128),
            buf(2, 256, 128), buf(2, 128, 128), buf(2, 128, 128), buf(NZ - 1, 2, 16, 128),
            buf(NY, 2, 256, 128),
            buf(QUART, ELL), buf(QUART, ELL), buf(2 * PART, ELL), buf(PART, ELL),
            buf(2, 2 * PART, ELL), buf(2, PART, ELL), buf(2, 2, 2, 256, 128), buf(2, 16 * EARLY, ELL), buf(LOCAL, ELL),
            buf(4, QUART, ELL, kind=BF16),
            buf(2, 2 * ELL, 2 * ELL, kind=BF16), buf(2, 2 * ELL, 2 * ELL, kind=BF16),
            buf(LOCAL, ELL, kind=BF16), buf(LOCAL, ELL, kind=BF16),
            buf(NZ, 2, 16, ELL), buf(NZ, 16, ELL), buf(NZ, 16, ELL), buf(NZ - 1, 16, ELL),
            buf(16, 8, 128),
            dma((2,)), dma((37,)), dma((4,)), dma((4,)), dma((4,)), dma((4,)), dma((2,)),
            dma, dma((5,)), dma((2,)), dma((4,)), dma((3,)), dma((3,)), dma, dma, dma((3,)), dma((3,)), dma((2,)), dma,
        ],
        compiler_params=pltpu.CompilerParams(
            collective_id=0, has_side_effects=True, vmem_limit_bytes=62 * 2**20
        ),
    )(expression, mixing)
    return basis, scores.T


def solution(mesh):
    return jax.shard_map(
        on_device,
        mesh=mesh,
        in_specs=(P("cell", "gene"), P()),
        out_specs=(P(None, "gene"), P("cell", "gene")),
        check_vma=False,
    )
```

```python
import jax
import jax.numpy as jnp
from jax import lax
from jax.experimental import pallas as pl
from jax.experimental.pallas import tpu as pltpu
from jax.sharding import PartitionSpec as P

GENES = 20480
CELLS = 4096
ELL = 256
NS_ITERS = 8
AHEAD = 2
NY, NX, NZ = 4, 4, 8
NYZ = NY * NZ
LOCAL = GENES // 16
QUART = LOCAL // NY
PART = LOCAL // 16
EARLY = PART * 7 // 10
MESH = pl.DeviceIdType.MESH
F32 = jnp.float32
BF16 = jnp.bfloat16
NT = (((1,), (1,)), ((), ()))
NN = (((1,), (0,)), ((), ()))
TN = (((0,), (0,)), ((), ()))


def hops(d, n):
    return min(d, n - d)


ALONG_Y = sorted(range(1, NY), key=lambda d: -hops(d, NY))
ALONG_Z = sorted(range(1, NZ), key=lambda d: -hops(d, NZ))
OTHERS = sorted(
    ((dy, dz) for dy in range(NY) for dz in range(NZ) if dy or dz),
    key=lambda d: -hops(d[0], NY) - hops(d[1], NZ),
)
PLANES = {
    2: sorted(
        ((dx, dy) for dx in range(2) for dy in range(NY) if dx or dy),
        key=lambda d: -d[0] - hops(d[1], NY),
    ),
    3: sorted(
        ((dx, dy) for dx in range(NX) for dy in range(NY) if dx or dy),
        key=lambda d: -hops(d[0], NX) - hops(d[1], NY),
    ),
}


def split(a):
    hi = a.astype(BF16)
    return hi, (a - hi.astype(F32)).astype(BF16)


def dot(a, b, dims):
    return lax.dot_general(a, b, dims, preferred_element_type=F32)


def dot2(a, b, dims):
    return dot(a, b[0], dims) + dot(a, b[1], dims)


def dot3(a, b, dims):
    return dot(a[0], b[0], dims) + (dot(a[0], b[1], dims) + dot(a[1], b[0], dims))


def joined(pair):
    return jnp.concatenate([pair[0], pair[1]], axis=1)


def halves(ref, block):
    ref[0] = block[:, :128]
    ref[1] = block[:, 128:]


def kernel(
    x_hbm, mix_hbm, basis_hbm, scores_ref,
    x_ref, mix_ref, basis_ref, xt, rx, part, corebuf, half, rsbuf, cellbuf, zbuf, total,
    selfp, selfcore, selfhalf, selfrs, selfall,
    low, high, quad, mid, pairbuf2, pairbuf3, pairself, early, final,
    stash, gh, gl, fh, fl, prod, prodcore, prodhalf, prodrs, sq,
    load_sem, send_sem, core_sem, rs_sem, ag_sem, cag_sem, z_sem,
    a2a_sem, self_sem, pair_sem, pself_sem, earlyx_sem, earlyy_sem, early_sem, fin_sem, finx_sem, finy_sem, pr_sem, sq_sem,
):
    cell, gene = lax.axis_index("cell"), lax.axis_index("gene")
    x, y = cell // NY, cell % NY
    z, c = gene // 2, gene % 2
    yz = y * NZ + z
    sends = []

    def put(src, dst, send, recv, to):
        copy = pltpu.make_async_remote_copy(
            src_ref=src, dst_ref=dst, send_sem=send, recv_sem=recv,
            device_id=to, device_id_type=MESH,
        )
        copy.start()
        return copy

    def taken(like, sem):
        pltpu.make_async_copy(like, like, sem).wait()

    def sent(like, sem):
        sends.append((like, sem))

    def at(dx, dy, dz):
        return (lax.rem(x + dx, NX) * NY + lax.rem(y + dy, NY), lax.rem(z + dz, NZ) * 2 + c)

    def paired(dx, dy):
        return ((x + dx * (1 - 2 * (x % 2))) * NY + lax.rem(y + dy, NY), gene)

    load_x = pltpu.make_async_copy(x_hbm, x_ref, load_sem.at[0])
    load_mix = pltpu.make_async_copy(mix_hbm, mix_ref, load_sem.at[1])
    load_x.start()
    load_mix.start()
    sibling = (cell, z * 2 + (1 - c))

    barrier = pltpu.get_barrier_semaphore()

    def greet(to):
        pl.semaphore_signal(barrier, inc=1, device_id=to, device_id_type=MESH)

    for d in ALONG_Z[:3]:
        greet(at(0, 0, d))
    for d in ALONG_Y:
        greet(at(0, d, 0))
    for d in ALONG_Z[3:]:
        greet(at(0, 0, d))
    for d in ALONG_Y:
        greet(at(d, 0, 0))
    greet(sibling)
    load_x.wait()

    for t in range(LOCAL // 128):
        xt[t * 128:(t + 1) * 128, :] = x_ref[:, t * 128:(t + 1) * 128].astype(F32).T
    own = pl.ds(pl.multiple_of(y * QUART, QUART), QUART)
    rx[y] = xt[own, :]
    xb = x_ref[...]
    halves(selfp, dot(xb, xb, NT))
    pl.semaphore_wait(barrier, NZ - 1 + NY - 1 + NX - 1 + 1)

    for i in ALONG_Y:
        q = lax.rem(y + i, NY)
        put(
            xt.at[pl.ds(pl.multiple_of(q * QUART, QUART), QUART), :], rx.at[y],
            send_sem.at[0], a2a_sem, (x * NY + q, gene),
        )
    sent(xt.at[pl.ds(0, 3 * QUART), :], send_sem.at[0])

    def rows(base, count):
        return pl.ds(pl.multiple_of(base, count), count)

    mine = rows(c * 128, 128)
    theirs = rows((1 - c) * 128, 128)

    put(selfp.at[:, theirs, :], selfcore, send_sem.at[1], self_sem.at[0], sibling)
    sent(selfcore, send_sem.at[1])
    taken(selfcore, self_sem.at[0])
    selfhalf[...] = selfp[:, mine, :] + selfcore[...]
    for i in ALONG_Z:
        k = lax.rem(z + i, NZ)
        put(
            selfhalf.at[:, rows(k * 16, 16), :], selfrs.at[i - 1],
            send_sem.at[2], self_sem.at[1], (cell, k * 2 + c),
        )
    sent(selfrs, send_sem.at[2])
    taken(selfrs, self_sem.at[1])
    piece = selfhalf[:, rows(z * 16, 16), :]
    for i in range(NZ - 1):
        piece = piece + selfrs[i]
    place = rows(c * 128 + z * 16, 16)
    selfall[y, :, place, :] = piece
    for i in ALONG_Z:
        k = lax.rem(z + i, NZ)
        put(
            selfall.at[y, :, place, :], selfall.at[y, :, place, :],
            send_sem.at[3], self_sem.at[2], (cell, k * 2 + c),
        )
    sent(selfrs, send_sem.at[3])
    taken(selfrs, self_sem.at[2])
    for i in ALONG_Y:
        q = lax.rem(y + i, NY)
        put(
            selfall.at[y, :, mine, :], selfall.at[y, :, mine, :],
            send_sem.at[4], self_sem.at[3], (x * NY + q, gene),
        )
    sent(selfall.at[pl.ds(0, 3), :, pl.ds(0, 128), :], send_sem.at[4])

    taken(rx.at[pl.ds(0, 3)], a2a_sem)

    def reduced(level, at_block, count, cross, scattering=None, summing=None, gathering=None):
        block = pl.ds(at_block, count)
        sem = 5 + 5 * level
        cross(1 - c)
        put(
            part.at[block, :, theirs, :], corebuf.at[block],
            send_sem.at[sem], core_sem.at[level], sibling,
        )
        sent(corebuf.at[block], send_sem.at[sem])
        cross(c)
        taken(corebuf.at[block], core_sem.at[level])
        half[block] = part[block, :, mine, :] + corebuf[block]
        if level < 2:
            for dy, dz in OTHERS:
                k = lax.rem(y + dy, NY) * NZ + lax.rem(z + dz, NZ)
                put(
                    half.at[block, k // 16, rows((k % 16) * 8, 8), :],
                    rsbuf.at[dy * NZ + dz - 1, block],
                    send_sem.at[sem + 1], rs_sem.at[level], at(0, dy, dz),
                )
            sent(rsbuf.at[:, block], send_sem.at[sem + 1])
            if scattering is not None:
                scattering()
            taken(rsbuf.at[:, block], rs_sem.at[level])
            tile = half[block, yz // 16, rows((yz % 16) * 8, 8), :]
            for i in range(NYZ - 1):
                tile = tile + rsbuf[i, block]
            piece = total.at[block, yz // 16, rows(c * 128 + (yz % 16) * 8, 8), :]
            piece[...] = tile
            for dy, dz in OTHERS:
                put(piece, piece, send_sem.at[sem + 3], ag_sem.at[level], at(0, dy, dz))
            sent(rsbuf.at[:, block], send_sem.at[sem + 3])
            if gathering is not None:
                gathering()
            taken(rsbuf.at[:, block], ag_sem.at[level])
        else:
            slot = level - 2
            peers = PLANES[level]
            strip = 128 // (len(peers) + 1)
            inbox = cellbuf.at[slot, pl.ds(0, len(peers)), :, pl.ds(0, strip), :]
            whose = (lambda dx, dy: paired(dx, dy)) if level == 2 else (lambda dx, dy: at(dx, dy, 0))
            index = (lambda to: to % 8) if level == 2 else (lambda to: to)
            own = half[at_block, :, rows(index(cell) * strip, strip), :]
            for dx, dy in peers:
                to = whose(dx, dy)
                put(
                    half.at[at_block, :, rows(index(to[0]) * strip, strip), :],
                    cellbuf.at[slot, dx * NY + dy - 1, :, pl.ds(0, strip), :],
                    send_sem.at[sem + 1], rs_sem.at[level], to,
                )
            sent(inbox, send_sem.at[sem + 1])
            taken(inbox, rs_sem.at[level])
            for i in range(len(peers)):
                own = own + cellbuf[slot, i, :, :strip, :]
            share = zbuf.at[slot, z, :, pl.ds(0, strip), :]
            share[...] = own
            for dz in ALONG_Z:
                put(share, share, send_sem.at[sem + 2], z_sem.at[slot], at(0, 0, dz))
            inbox = zbuf.at[slot, pl.ds(0, NZ - 1), :, pl.ds(0, strip), :]
            sent(inbox, send_sem.at[sem + 2])
            if summing is not None:
                summing()
            taken(inbox, z_sem.at[slot])
            own = zbuf[slot, 0, :, :strip, :]
            for i in range(1, NZ):
                own = own + zbuf[slot, i, :, :strip, :]
            piece = total.at[at_block, :, rows(c * 128 + index(cell) * strip, strip), :]
            piece[...] = own
            for dx, dy in peers:
                put(piece, piece, send_sem.at[sem + 3], ag_sem.at[level], whose(dx, dy))
            inbox = cellbuf.at[slot, pl.ds(0, len(peers)), :, pl.ds(0, strip), :]
            sent(inbox, send_sem.at[sem + 3])
            gathering()
            taken(inbox, ag_sem.at[level])
        put(
            total.at[block, :, mine, :], total.at[block, :, mine, :],
            send_sem.at[sem + 4], cag_sem.at[level], sibling,
        )
        sent(corebuf.at[block], send_sem.at[sem + 4])
        taken(corebuf.at[block], cag_sem.at[level])

    def prepare(level, lower, upper, slot=0):
        for at_row, gram in ((0, lower), (ELL, upper)):
            spot = slice(at_row, at_row + ELL)
            gh[slot, spot, spot], gl[slot, spot, spot] = split(gram)
        mix = mix_ref[level]
        first = dot2(mix[:, :ELL], (gh[slot, :ELL, :ELL], gl[slot, :ELL, :ELL]), NN)
        second = dot2(mix[:, ELL:], (gh[slot, ELL:, ELL:], gl[slot, ELL:, ELL:]), NN)
        squares = jnp.sum(lower * lower, keepdims=True) + jnp.sum(upper * upper, keepdims=True)
        return first, second, squares

    def weights(level, cross, ready, slot=0):
        first, second, squares = ready
        inv = 1.0 / jnp.sqrt(squares + 2.0 * jnp.sum(cross * cross, keepdims=True) + 1e-06)
        over, under = split(cross), split(cross.T)
        gh[slot, :ELL, ELL:], gl[slot, :ELL, ELL:] = over
        gh[slot, ELL:, :ELL], gl[slot, ELL:, :ELL] = under
        mix = mix_ref[level]
        once = jnp.concatenate(
            [first + dot2(mix[:, ELL:], under, NN), second + dot2(mix[:, :ELL], over, NN)], axis=1
        )
        twice = dot3(split(once), (gh[slot], gl[slot]), NN)
        return 0.5 * mix.astype(F32) + once * inv - (0.5 * twice) * (inv * inv)

    def own_gram(w, slot=0):
        return dot3(split(dot3(w, (gh[slot], gl[slot]), NN)), w, NT)

    def left(w):
        return w[0][:, :ELL], w[1][:, :ELL]

    def right(w):
        return w[0][:, ELL:], w[1][:, ELL:]

    def stashed(base, count):
        at_rows = rows(base, count) if base is not None else pl.ds(0, count)
        return (stash[0, at_rows, :], stash[1, at_rows, :]), (stash[2, at_rows, :], stash[3, at_rows, :])

    def sketched(w, base, count):
        lower, upper = stashed(base, count)
        return dot3(lower, left(w), NT) + dot3(upper, right(w), NT)

    def crossed(at_block, count):
        def cross(side):
            side_rows = rows(side * 128, 128)
            lower = stash[0, :count, side_rows], stash[1, :count, side_rows]
            block = dot3(lower, stashed(None, count)[1], TN)
            part[at_block, 0, side_rows, :] = block[:, :128]
            part[at_block, 1, side_rows, :] = block[:, 128:]

        return cross

    def keep(lower, upper):
        count = lower.shape[0]
        stash[0, :count], stash[1, :count] = split(lower)
        stash[2, :count], stash[3, :count] = split(upper)

    for i in range(NY):
        stash[i] = rx[i].astype(BF16)

    def cross_batches(side):
        side_rows = rows(side * 128, 128)
        for p in range(2):
            block = dot(stash[2 * p, :, side_rows], stash[2 * p + 1], TN)
            part[p, 0, side_rows, :] = block[:, :128]
            part[p, 1, side_rows, :] = block[:, 128:]

    ready = []

    def swap_selves():
        taken(selfall.at[pl.ds(0, 3), :, pl.ds(0, 128), :], self_sem.at[3])
        put(
            selfall.at[:, :, mine, :], selfall.at[:, :, mine, :],
            send_sem.at[25], self_sem.at[4], sibling,
        )
        sent(selfall.at[:, :, pl.ds(0, 128), :], send_sem.at[25])
        load_mix.wait()
        taken(selfall.at[:, :, pl.ds(0, 128), :], self_sem.at[4])
        for p in range(2):
            ready.append(prepare(0, joined(selfall[2 * p]), joined(selfall[2 * p + 1]), p))

    reduced(0, 0, 2, cross_batches, gathering=swap_selves)
    kept = []
    for p, sketch in ((0, low), (1, high)):
        w = split(weights(0, joined(total[p]), ready[p], p))
        sketch[...] = dot2(stash[2 * p], left(w), NT) + dot2(stash[2 * p + 1], right(w), NT)
        kept.append(w)

    keep(low[...], high[...])
    grams = []
    reduced(
        1, 2, 1, crossed(2, QUART),
        scattering=lambda: grams.extend(own_gram(kept[p], p) for p in range(2)),
        gathering=lambda: ready.append(prepare(1, *grams)),
    )
    w = split(weights(1, joined(total[2]), ready[-1]))

    def order(cx, cy):
        return cy * 4 + cx % 2 * 2 + cx // 2

    for level, step, src, buf in ((2, 1, quad, pairbuf2), (3, 2, mid, pairbuf3)):
        slot = level - 2
        bit = x // step % 2
        to = ((x + step * (1 - 2 * bit)) * NY + y, gene)
        count = buf.shape[1]
        src[...] = sketched(w, (1 - bit) * count, count)
        put(src, buf.at[bit], send_sem.at[26 + slot], pair_sem.at[slot], to)
        sent(buf.at[0], send_sem.at[26 + slot])
        buf[bit] = sketched(w, bit * count, count)
        halves(pairself.at[slot, bit], own_gram(w))
        share = pairself.at[slot, bit, :, mine, :]
        put(share, share, send_sem.at[28 + slot], pself_sem.at[slot], to)
        sent(pairself.at[slot, 0, :, pl.ds(0, 128), :], send_sem.at[28 + slot])

        def summing():
            here = early.at[:, rows(order(x, y) * EARLY, EARLY), :]
            here[...] = buf[:, :EARLY, :]
            for d in ALONG_Y:
                put(here, here, send_sem.at[36], earlyx_sem.at[d - 1], at(d, 0, 0))
                put(here, here, send_sem.at[36], earlyy_sem.at[d - 1], at(0, d, 0))
            sent(early.at[:, pl.ds(0, 15 * EARLY), :], send_sem.at[36])

        def gathering():
            taken(pairself.at[slot, 0, :, pl.ds(0, 128), :], pself_sem.at[slot])
            across = pairself.at[slot, 1 - bit, :, mine, :]
            put(across, across, send_sem.at[30 + slot], pself_sem.at[2 + slot], sibling)
            sent(pairself.at[slot, 0, :, pl.ds(0, 128), :], send_sem.at[30 + slot])
            if level == 3:
                for d in (1, 3, 2):
                    cx, cy = lax.rem(x + NX - d, NX), lax.rem(y + NY - d, NY)
                    taken(early.at[:, pl.ds(0, EARLY), :], earlyx_sem.at[d - 1])
                    first = early.at[0, rows(order(cx, y) * EARLY, EARLY), :]
                    for e in ALONG_Y:
                        put(first, first, send_sem.at[36], early_sem, at(0, e, 0))
                    taken(early.at[:, pl.ds(0, EARLY), :], earlyy_sem.at[d - 1])
                    second = early.at[1, rows(order(x, cy) * EARLY, EARLY), :]
                    for e in ALONG_Y:
                        put(second, second, send_sem.at[36], early_sem, at(e, 0, 0))
            taken(pairself.at[slot, 0, :, pl.ds(0, 128), :], pself_sem.at[2 + slot])
            ready.append(prepare(level, joined(pairself[slot, 0]), joined(pairself[slot, 1])))

        taken(buf.at[0], pair_sem.at[slot])
        keep(buf[0], buf[1])
        reduced(
            level, level + 1, 1, crossed(level + 1, count),
            summing=summing if level == 3 else None, gathering=gathering,
        )
        w = split(weights(level, joined(total[level + 1]), ready[-1]))

    def chunk(cx, cy, skip, count):
        return final.at[pl.ds(pl.multiple_of(order(cx, cy) * PART + EARLY + skip, 8), count), :]

    late = PART - EARLY
    cut = (late // 8 + 1) // 2 * 8
    here = chunk(x, y, 0, late)
    here[...] = sketched(w, None, PART)[EARLY:]
    for d in ALONG_Y:
        put(here, here, send_sem.at[32], finx_sem.at[d - 1], at(d, 0, 0))
        put(here, here, send_sem.at[32], finy_sem.at[d - 1], at(0, d, 0))
    sent(final.at[pl.ds(0, 15 * late), :], send_sem.at[32])

    gram = own_gram(w)
    norm = jnp.sqrt(jnp.sum(gram * gram, keepdims=True) + 1e-06)
    eye = (
        lax.broadcasted_iota(jnp.int32, (ELL, ELL), 0) == lax.broadcasted_iota(jnp.int32, (ELL, ELL), 1)
    ).astype(F32)
    ymat = gram * (1.0 / norm)
    middle = 1.5 * eye - 0.5 * ymat
    zmat = middle
    ymat = dot3(split(ymat), split(middle), NN)

    def refine(step, carry):
        ymat, zmat = split(carry[0]), split(carry[1])
        middle = split(1.5 * eye - 0.5 * dot3(zmat, ymat, NN))
        return dot3(ymat, middle, NN), dot3(middle, zmat, NN)

    ymat, zmat = lax.fori_loop(0, AHEAD, refine, (ymat, zmat))

    for d in (1, 3, 2):
        cx, cy = lax.rem(x + NX - d, NX), lax.rem(y + NY - d, NY)
        taken(here, finx_sem.at[d - 1])
        first = chunk(cx, y, 0, cut)
        for e in ALONG_Y:
            put(first, first, send_sem.at[32], fin_sem, at(0, e, 0))
        taken(here, finy_sem.at[d - 1])
        second = chunk(x, cy, cut, late - cut)
        for e in ALONG_Y:
            put(second, second, send_sem.at[32], fin_sem, at(e, 0, 0))

    taken(final.at[pl.ds(0, 18 * EARLY), :], early_sem)
    ahead = dot3(split(early[0]), left(w), NT) + dot3(split(early[1]), right(w), NT)
    for k in range(16):
        final[k * PART:k * PART + EARLY, :] = ahead[k * EARLY:(k + 1) * EARLY]

    ymat, zmat = lax.fori_loop(AHEAD, NS_ITERS - 2, refine, (ymat, zmat))
    ymat, zmat = split(ymat), split(zmat)
    middle = split(1.5 * eye - 0.5 * dot3(zmat, ymat, NN))
    scaled = split(dot3(middle, zmat, NN) * (jnp.sqrt(F32(GENES)) / jnp.sqrt(norm)))

    taken(final.at[pl.ds(0, 9 * late), :], fin_sem)
    hi, lo = split(final[...])
    fh[...] = hi
    fl[...] = lo
    shares = dot2(x_ref[...], (fh[...], fl[...]), NN)
    prod[...] = dot3(scaled, split(shares), NT).reshape(NZ, 2, 16, ELL)

    put(prod.at[:, 1 - c], prodcore, send_sem.at[33], pr_sem.at[0], sibling)
    sent(prodcore, send_sem.at[33])
    taken(prodcore, pr_sem.at[0])
    prodhalf[...] = prod[:, c] + prodcore[...]
    for i in ALONG_Z:
        k = lax.rem(z + i, NZ)
        put(prodhalf.at[k], prodrs.at[i - 1], send_sem.at[34], pr_sem.at[1], (cell, k * 2 + c))
    sent(prodrs, send_sem.at[34])
    basis_ref[...] = dot3(scaled, (fh[...], fl[...]), NT)
    store_basis = pltpu.make_async_copy(basis_ref, basis_hbm, load_sem.at[0])
    store_basis.start()
    taken(prodrs, pr_sem.at[1])
    scores = prodhalf[z]
    for i in range(NZ - 1):
        scores = scores + prodrs[i]
    squares = jnp.sum(scores * scores, axis=1, keepdims=True)
    lane = lax.broadcasted_iota(jnp.int32, (8, 128), 1)
    sq[cell] = jnp.where(
        lane < 64, jnp.broadcast_to(squares[:8], (8, 128)), jnp.broadcast_to(squares[8:], (8, 128))
    )
    for dx, dy in PLANES[3]:
        put(sq.at[cell], sq.at[cell], send_sem.at[35], sq_sem, at(dx, dy, 0))
    sent(sq.at[pl.ds(0, 15)], send_sem.at[35])
    taken(sq.at[pl.ds(0, 15)], sq_sem)
    squares = jnp.sum(sq[...], axis=0)
    spread = jnp.concatenate([squares[:, :1], squares[:, 64:65]], axis=0) * (1.0 / CELLS)
    scores_ref[...] = scores / jnp.sqrt(spread + 1e-05)
    store_basis.wait()
    for like, sem in sends:
        taken(like, sem)


def on_device(expression, mixing):
    vmem = pl.BlockSpec(memory_space=pltpu.VMEM)
    dma = pltpu.SemaphoreType.DMA

    def buf(*shape, kind=F32):
        return pltpu.VMEM(shape, kind)

    basis, scores = pl.pallas_call(
        kernel,
        out_shape=(
            jax.ShapeDtypeStruct((ELL, LOCAL), F32),
            jax.ShapeDtypeStruct((16, ELL), F32),
        ),
        in_specs=[pl.BlockSpec(memory_space=pltpu.HBM)] * 2,
        out_specs=(pl.BlockSpec(memory_space=pltpu.HBM), vmem),
        scratch_shapes=[
            buf(ELL, LOCAL, kind=BF16), buf(4, ELL, 2 * ELL, kind=BF16), buf(ELL, LOCAL),
            buf(LOCAL, ELL), buf(NY, QUART, ELL), buf(5, 2, 256, 128), buf(5, 2, 128, 128),
            buf(5, 2, 128, 128), buf(NYZ - 1, 5, 8, 128), buf(2, 15, 2, 16, 128), buf(2, NZ, 2, 16, 128), buf(5, 2, 256, 128),
            buf(2, 256, 128), buf(2, 128, 128), buf(2, 128, 128), buf(NZ - 1, 2, 16, 128),
            buf(NY, 2, 256, 128),
            buf(QUART, ELL), buf(QUART, ELL), buf(2 * PART, ELL), buf(PART, ELL),
            buf(2, 2 * PART, ELL), buf(2, PART, ELL), buf(2, 2, 2, 256, 128), buf(2, 16 * EARLY, ELL), buf(LOCAL, ELL),
            buf(4, QUART, ELL, kind=BF16),
            buf(2, 2 * ELL, 2 * ELL, kind=BF16), buf(2, 2 * ELL, 2 * ELL, kind=BF16),
            buf(LOCAL, ELL, kind=BF16), buf(LOCAL, ELL, kind=BF16),
            buf(NZ, 2, 16, ELL), buf(NZ, 16, ELL), buf(NZ, 16, ELL), buf(NZ - 1, 16, ELL),
            buf(16, 8, 128),
            dma((2,)), dma((37,)), dma((4,)), dma((4,)), dma((4,)), dma((4,)), dma((2,)),
            dma, dma((5,)), dma((2,)), dma((4,)), dma((3,)), dma((3,)), dma, dma, dma((3,)), dma((3,)), dma((2,)), dma,
        ],
        compiler_params=pltpu.CompilerParams(
            collective_id=0, has_side_effects=True, vmem_limit_bytes=62 * 2**20
        ),
    )(expression, mixing)
    return basis, scores.T


def solution(mesh):
    return jax.shard_map(
        on_device,
        mesh=mesh,
        in_specs=(P("cell", "gene"), P()),
        out_specs=(P(None, "gene"), P("cell", "gene")),
        check_vma=False,
    )
```

```python
import jax
import jax.numpy as jnp
from jax import lax
from jax.experimental import pallas as pl
from jax.experimental.pallas import tpu as pltpu
from jax.sharding import PartitionSpec as P

GENES = 20480
CELLS = 4096
ELL = 256
NS_ITERS = 8
AHEAD = 2
STRIPS = 8
NY, NX, NZ = 4, 4, 8
NYZ = NY * NZ
LOCAL = GENES // 16
QUART = LOCAL // NY
PART = LOCAL // 16
EARLY = PART * 7 // 10
MESH = pl.DeviceIdType.MESH
F32 = jnp.float32
BF16 = jnp.bfloat16
NT = (((1,), (1,)), ((), ()))
NN = (((1,), (0,)), ((), ()))
TN = (((0,), (0,)), ((), ()))


def hops(d, n):
    return min(d, n - d)


ALONG_Y = sorted(range(1, NY), key=lambda d: -hops(d, NY))
ALONG_Z = sorted(range(1, NZ), key=lambda d: -hops(d, NZ))
OTHERS = sorted(
    ((dy, dz) for dy in range(NY) for dz in range(NZ) if dy or dz),
    key=lambda d: -hops(d[0], NY) - hops(d[1], NZ),
)
PLANES = {
    2: sorted(
        ((dx, dy) for dx in range(2) for dy in range(NY) if dx or dy),
        key=lambda d: -d[0] - hops(d[1], NY),
    ),
    3: sorted(
        ((dx, dy) for dx in range(NX) for dy in range(NY) if dx or dy),
        key=lambda d: -hops(d[0], NX) - hops(d[1], NY),
    ),
}


def split(a):
    hi = a.astype(BF16)
    return hi, (a - hi.astype(F32)).astype(BF16)


def dot(a, b, dims):
    return lax.dot_general(a, b, dims, preferred_element_type=F32)


def dot2(a, b, dims):
    return dot(a, b[0], dims) + dot(a, b[1], dims)


def dot3(a, b, dims):
    return dot(a[0], b[0], dims) + (dot(a[0], b[1], dims) + dot(a[1], b[0], dims))


def joined(pair):
    return jnp.concatenate([pair[0], pair[1]], axis=1)


def halves(ref, block):
    ref[0] = block[:, :128]
    ref[1] = block[:, 128:]


def kernel(
    x_hbm, mix_hbm, basis_hbm, scores_ref,
    x_ref, mix_ref, basis_ref, xt, rx, part, corebuf, half, rsbuf, cellbuf, zbuf, total,
    selfp, selfcore, selfhalf, selfrs, selfall,
    low, high, quad, mid, pairbuf2, pairbuf3, pairself, early, final,
    stash, gh, gl, fh, fl, prod, prodcore, prodhalf, prodrs, sq,
    load_sem, send_sem, core_sem, rs_sem, ag_sem, cag_sem, z_sem,
    a2a_sem, self_sem, pair_sem, pself_sem, earlyx_sem, earlyy_sem, early_sem, fin_sem, finx_sem, finy_sem, pr_sem, sq_sem,
):
    cell, gene = lax.axis_index("cell"), lax.axis_index("gene")
    x, y = cell // NY, cell % NY
    z, c = gene // 2, gene % 2
    yz = y * NZ + z
    sends = []

    def put(src, dst, send, recv, to):
        copy = pltpu.make_async_remote_copy(
            src_ref=src, dst_ref=dst, send_sem=send, recv_sem=recv,
            device_id=to, device_id_type=MESH,
        )
        copy.start()
        return copy

    def taken(like, sem):
        pltpu.make_async_copy(like, like, sem).wait()

    def sent(like, sem):
        sends.append((like, sem))

    def at(dx, dy, dz):
        return (lax.rem(x + dx, NX) * NY + lax.rem(y + dy, NY), lax.rem(z + dz, NZ) * 2 + c)

    def paired(dx, dy):
        return ((x + dx * (1 - 2 * (x % 2))) * NY + lax.rem(y + dy, NY), gene)

    load_x = pltpu.make_async_copy(x_hbm, x_ref, load_sem.at[0])
    load_mix = pltpu.make_async_copy(mix_hbm, mix_ref, load_sem.at[1])
    load_x.start()
    load_mix.start()
    sibling = (cell, z * 2 + (1 - c))

    barrier = pltpu.get_barrier_semaphore()

    def greet(to):
        pl.semaphore_signal(barrier, inc=1, device_id=to, device_id_type=MESH)

    for d in ALONG_Z[:3]:
        greet(at(0, 0, d))
    for d in ALONG_Y:
        greet(at(0, d, 0))
    for d in ALONG_Z[3:]:
        greet(at(0, 0, d))
    for d in ALONG_Y:
        greet(at(d, 0, 0))
    greet(sibling)
    load_x.wait()

    for t in range(LOCAL // 128):
        xt[t * 128:(t + 1) * 128, :] = x_ref[:, t * 128:(t + 1) * 128].astype(F32).T
    own = pl.ds(pl.multiple_of(y * QUART, QUART), QUART)
    rx[y] = xt[own, :]
    xb = x_ref[...]
    halves(selfp, dot(xb, xb, NT))
    pl.semaphore_wait(barrier, NZ - 1 + NY - 1 + NX - 1 + 1)

    for i in ALONG_Y:
        q = lax.rem(y + i, NY)
        put(
            xt.at[pl.ds(pl.multiple_of(q * QUART, QUART), QUART), :], rx.at[y],
            send_sem.at[0], a2a_sem, (x * NY + q, gene),
        )
    sent(xt.at[pl.ds(0, 3 * QUART), :], send_sem.at[0])

    def rows(base, count):
        return pl.ds(pl.multiple_of(base, count), count)

    mine = rows(c * 128, 128)
    theirs = rows((1 - c) * 128, 128)

    put(selfp.at[:, theirs, :], selfcore, send_sem.at[1], self_sem.at[0], sibling)
    sent(selfcore, send_sem.at[1])
    taken(selfcore, self_sem.at[0])
    selfhalf[...] = selfp[:, mine, :] + selfcore[...]
    for i in ALONG_Z:
        k = lax.rem(z + i, NZ)
        put(
            selfhalf.at[:, rows(k * 16, 16), :], selfrs.at[i - 1],
            send_sem.at[2], self_sem.at[1], (cell, k * 2 + c),
        )
    sent(selfrs, send_sem.at[2])
    taken(selfrs, self_sem.at[1])
    piece = selfhalf[:, rows(z * 16, 16), :]
    for i in range(NZ - 1):
        piece = piece + selfrs[i]
    place = rows(c * 128 + z * 16, 16)
    selfall[y, :, place, :] = piece
    for i in ALONG_Z:
        k = lax.rem(z + i, NZ)
        put(
            selfall.at[y, :, place, :], selfall.at[y, :, place, :],
            send_sem.at[3], self_sem.at[2], (cell, k * 2 + c),
        )
    sent(selfrs, send_sem.at[3])
    taken(selfrs, self_sem.at[2])
    for i in ALONG_Y:
        q = lax.rem(y + i, NY)
        put(
            selfall.at[y, :, mine, :], selfall.at[y, :, mine, :],
            send_sem.at[4], self_sem.at[3], (x * NY + q, gene),
        )
    sent(selfall.at[pl.ds(0, 3), :, pl.ds(0, 128), :], send_sem.at[4])

    taken(rx.at[pl.ds(0, 3)], a2a_sem)

    def reduced(level, at_block, count, cross, scattering=None, summing=None, gathering=None):
        block = pl.ds(at_block, count)
        sem = 5 + 5 * level
        cross(1 - c)
        put(
            part.at[block, :, theirs, :], corebuf.at[block],
            send_sem.at[sem], core_sem.at[level], sibling,
        )
        sent(corebuf.at[block], send_sem.at[sem])
        cross(c)
        taken(corebuf.at[block], core_sem.at[level])
        half[block] = part[block, :, mine, :] + corebuf[block]
        if level < 2:
            for dy, dz in OTHERS:
                k = lax.rem(y + dy, NY) * NZ + lax.rem(z + dz, NZ)
                put(
                    half.at[block, k // 16, rows((k % 16) * 8, 8), :],
                    rsbuf.at[dy * NZ + dz - 1, block],
                    send_sem.at[sem + 1], rs_sem.at[level], at(0, dy, dz),
                )
            sent(rsbuf.at[:, block], send_sem.at[sem + 1])
            if scattering is not None:
                scattering()
            taken(rsbuf.at[:, block], rs_sem.at[level])
            tile = half[block, yz // 16, rows((yz % 16) * 8, 8), :]
            for i in range(NYZ - 1):
                tile = tile + rsbuf[i, block]
            piece = total.at[block, yz // 16, rows(c * 128 + (yz % 16) * 8, 8), :]
            piece[...] = tile
            for dy, dz in OTHERS:
                put(piece, piece, send_sem.at[sem + 3], ag_sem.at[level], at(0, dy, dz))
            sent(rsbuf.at[:, block], send_sem.at[sem + 3])
            if gathering is not None:
                gathering()
            taken(rsbuf.at[:, block], ag_sem.at[level])
        else:
            slot = level - 2
            peers = PLANES[level]
            strip = 128 // (len(peers) + 1)
            inbox = cellbuf.at[slot, pl.ds(0, len(peers)), :, pl.ds(0, strip), :]
            whose = (lambda dx, dy: paired(dx, dy)) if level == 2 else (lambda dx, dy: at(dx, dy, 0))
            index = (lambda to: to % 8) if level == 2 else (lambda to: to)
            own = half[at_block, :, rows(index(cell) * strip, strip), :]
            for dx, dy in peers:
                to = whose(dx, dy)
                put(
                    half.at[at_block, :, rows(index(to[0]) * strip, strip), :],
                    cellbuf.at[slot, dx * NY + dy - 1, :, pl.ds(0, strip), :],
                    send_sem.at[sem + 1], rs_sem.at[level], to,
                )
            sent(inbox, send_sem.at[sem + 1])
            taken(inbox, rs_sem.at[level])
            for i in range(len(peers)):
                own = own + cellbuf[slot, i, :, :strip, :]
            share = zbuf.at[slot, z, :, pl.ds(0, strip), :]
            share[...] = own
            for dz in ALONG_Z:
                put(share, share, send_sem.at[sem + 2], z_sem.at[slot], at(0, 0, dz))
            inbox = zbuf.at[slot, pl.ds(0, NZ - 1), :, pl.ds(0, strip), :]
            sent(inbox, send_sem.at[sem + 2])
            if summing is not None:
                summing()
            taken(inbox, z_sem.at[slot])
            own = zbuf[slot, 0, :, :strip, :]
            for i in range(1, NZ):
                own = own + zbuf[slot, i, :, :strip, :]
            piece = total.at[at_block, :, rows(c * 128 + index(cell) * strip, strip), :]
            piece[...] = own
            for dx, dy in peers:
                put(piece, piece, send_sem.at[sem + 3], ag_sem.at[level], whose(dx, dy))
            inbox = cellbuf.at[slot, pl.ds(0, len(peers)), :, pl.ds(0, strip), :]
            sent(inbox, send_sem.at[sem + 3])
            gathering()
            taken(inbox, ag_sem.at[level])
        put(
            total.at[block, :, mine, :], total.at[block, :, mine, :],
            send_sem.at[sem + 4], cag_sem.at[level], sibling,
        )
        sent(corebuf.at[block], send_sem.at[sem + 4])
        taken(corebuf.at[block], cag_sem.at[level])

    def prepare(level, lower, upper, slot=0):
        for at_row, gram in ((0, lower), (ELL, upper)):
            spot = slice(at_row, at_row + ELL)
            gh[slot, spot, spot], gl[slot, spot, spot] = split(gram)
        mix = mix_ref[level]
        first = dot2(mix[:, :ELL], (gh[slot, :ELL, :ELL], gl[slot, :ELL, :ELL]), NN)
        second = dot2(mix[:, ELL:], (gh[slot, ELL:, ELL:], gl[slot, ELL:, ELL:]), NN)
        squares = jnp.sum(lower * lower, keepdims=True) + jnp.sum(upper * upper, keepdims=True)
        return first, second, squares

    def weights(level, cross, ready, slot=0):
        first, second, squares = ready
        inv = 1.0 / jnp.sqrt(squares + 2.0 * jnp.sum(cross * cross, keepdims=True) + 1e-06)
        over, under = split(cross), split(cross.T)
        gh[slot, :ELL, ELL:], gl[slot, :ELL, ELL:] = over
        gh[slot, ELL:, :ELL], gl[slot, ELL:, :ELL] = under
        mix = mix_ref[level]
        once = jnp.concatenate(
            [first + dot2(mix[:, ELL:], under, NN), second + dot2(mix[:, :ELL], over, NN)], axis=1
        )
        twice = dot3(split(once), (gh[slot], gl[slot]), NN)
        return 0.5 * mix.astype(F32) + once * inv - (0.5 * twice) * (inv * inv)

    def own_gram(w, slot=0):
        return dot3(split(dot3(w, (gh[slot], gl[slot]), NN)), w, NT)

    def left(w):
        return w[0][:, :ELL], w[1][:, :ELL]

    def right(w):
        return w[0][:, ELL:], w[1][:, ELL:]

    def stashed(base, count):
        at_rows = rows(base, count) if base is not None else pl.ds(0, count)
        return (stash[0, at_rows, :], stash[1, at_rows, :]), (stash[2, at_rows, :], stash[3, at_rows, :])

    def sketched(w, base, count):
        lower, upper = stashed(base, count)
        return dot3(lower, left(w), NT) + dot3(upper, right(w), NT)

    def crossed(at_block, count):
        def cross(side):
            side_rows = rows(side * 128, 128)
            lower = stash[0, :count, side_rows], stash[1, :count, side_rows]
            block = dot3(lower, stashed(None, count)[1], TN)
            part[at_block, 0, side_rows, :] = block[:, :128]
            part[at_block, 1, side_rows, :] = block[:, 128:]

        return cross

    def keep(lower, upper):
        count = lower.shape[0]
        stash[0, :count], stash[1, :count] = split(lower)
        stash[2, :count], stash[3, :count] = split(upper)

    for i in range(NY):
        stash[i] = rx[i].astype(BF16)

    def cross_batches(side):
        side_rows = rows(side * 128, 128)
        for p in range(2):
            block = dot(stash[2 * p, :, side_rows], stash[2 * p + 1], TN)
            part[p, 0, side_rows, :] = block[:, :128]
            part[p, 1, side_rows, :] = block[:, 128:]

    ready = []

    def swap_selves():
        taken(selfall.at[pl.ds(0, 3), :, pl.ds(0, 128), :], self_sem.at[3])
        put(
            selfall.at[:, :, mine, :], selfall.at[:, :, mine, :],
            send_sem.at[25], self_sem.at[4], sibling,
        )
        sent(selfall.at[:, :, pl.ds(0, 128), :], send_sem.at[25])
        load_mix.wait()
        taken(selfall.at[:, :, pl.ds(0, 128), :], self_sem.at[4])
        for p in range(2):
            ready.append(prepare(0, joined(selfall[2 * p]), joined(selfall[2 * p + 1]), p))

    reduced(0, 0, 2, cross_batches, gathering=swap_selves)
    kept = []
    for p, sketch in ((0, low), (1, high)):
        w = split(weights(0, joined(total[p]), ready[p], p))
        sketch[...] = dot2(stash[2 * p], left(w), NT) + dot2(stash[2 * p + 1], right(w), NT)
        kept.append(w)

    keep(low[...], high[...])
    grams = []
    reduced(
        1, 2, 1, crossed(2, QUART),
        scattering=lambda: grams.extend(own_gram(kept[p], p) for p in range(2)),
        gathering=lambda: ready.append(prepare(1, *grams)),
    )
    w = split(weights(1, joined(total[2]), ready[-1]))

    def order(cx, cy):
        return cy * 4 + cx % 2 * 2 + cx // 2

    for level, step, src, buf in ((2, 1, quad, pairbuf2), (3, 2, mid, pairbuf3)):
        slot = level - 2
        bit = x // step % 2
        to = ((x + step * (1 - 2 * bit)) * NY + y, gene)
        count = buf.shape[1]
        src[...] = sketched(w, (1 - bit) * count, count)
        put(src, buf.at[bit], send_sem.at[26 + slot], pair_sem.at[slot], to)
        sent(buf.at[0], send_sem.at[26 + slot])
        buf[bit] = sketched(w, bit * count, count)
        halves(pairself.at[slot, bit], own_gram(w))
        share = pairself.at[slot, bit, :, mine, :]
        put(share, share, send_sem.at[28 + slot], pself_sem.at[slot], to)
        sent(pairself.at[slot, 0, :, pl.ds(0, 128), :], send_sem.at[28 + slot])

        def summing():
            here = early.at[:, rows(order(x, y) * EARLY, EARLY), :]
            here[...] = buf[:, :EARLY, :]
            for d in ALONG_Y:
                put(here, here, send_sem.at[36], earlyx_sem.at[d - 1], at(d, 0, 0))
                put(here, here, send_sem.at[36], earlyy_sem.at[d - 1], at(0, d, 0))
            sent(early.at[:, pl.ds(0, 15 * EARLY), :], send_sem.at[36])

        def gathering():
            taken(pairself.at[slot, 0, :, pl.ds(0, 128), :], pself_sem.at[slot])
            across = pairself.at[slot, 1 - bit, :, mine, :]
            put(across, across, send_sem.at[30 + slot], pself_sem.at[2 + slot], sibling)
            sent(pairself.at[slot, 0, :, pl.ds(0, 128), :], send_sem.at[30 + slot])
            if level == 3:
                for d in (1, 3, 2):
                    cx, cy = lax.rem(x + NX - d, NX), lax.rem(y + NY - d, NY)
                    taken(early.at[:, pl.ds(0, EARLY), :], earlyx_sem.at[d - 1])
                    first = early.at[0, rows(order(cx, y) * EARLY, EARLY), :]
                    for e in ALONG_Y:
                        put(first, first, send_sem.at[36], early_sem, at(0, e, 0))
                    taken(early.at[:, pl.ds(0, EARLY), :], earlyy_sem.at[d - 1])
                    second = early.at[1, rows(order(x, cy) * EARLY, EARLY), :]
                    for e in ALONG_Y:
                        put(second, second, send_sem.at[36], early_sem, at(e, 0, 0))
            taken(pairself.at[slot, 0, :, pl.ds(0, 128), :], pself_sem.at[2 + slot])
            ready.append(prepare(level, joined(pairself[slot, 0]), joined(pairself[slot, 1])))

        taken(buf.at[0], pair_sem.at[slot])
        keep(buf[0], buf[1])
        reduced(
            level, level + 1, 1, crossed(level + 1, count),
            summing=summing if level == 3 else None, gathering=gathering,
        )
        w = split(weights(level, joined(total[level + 1]), ready[-1]))

    def chunk(cx, cy, skip, count):
        return final.at[pl.ds(pl.multiple_of(order(cx, cy) * PART + EARLY + skip, 8), count), :]

    late = PART - EARLY
    cut = (late // 8 + 1) // 2 * 8
    here = chunk(x, y, 0, late)
    here[...] = sketched(w, None, PART)[EARLY:]
    for d in ALONG_Y:
        put(here, here, send_sem.at[32], finx_sem.at[d - 1], at(d, 0, 0))
        put(here, here, send_sem.at[32], finy_sem.at[d - 1], at(0, d, 0))
    sent(final.at[pl.ds(0, 15 * late), :], send_sem.at[32])

    gram = own_gram(w)
    norm = jnp.sqrt(jnp.sum(gram * gram, keepdims=True) + 1e-06)
    eye = (
        lax.broadcasted_iota(jnp.int32, (ELL, ELL), 0) == lax.broadcasted_iota(jnp.int32, (ELL, ELL), 1)
    ).astype(F32)
    ymat = gram * (1.0 / norm)
    middle = 1.5 * eye - 0.5 * ymat
    zmat = middle
    ymat = dot3(split(ymat), split(middle), NN)

    def refine(step, carry):
        ymat, zmat = split(carry[0]), split(carry[1])
        middle = split(1.5 * eye - 0.5 * dot3(zmat, ymat, NN))
        return dot3(ymat, middle, NN), dot3(middle, zmat, NN)

    ymat, zmat = lax.fori_loop(0, AHEAD, refine, (ymat, zmat))

    for d in (1, 3, 2):
        cx, cy = lax.rem(x + NX - d, NX), lax.rem(y + NY - d, NY)
        taken(here, finx_sem.at[d - 1])
        first = chunk(cx, y, 0, cut)
        for e in ALONG_Y:
            put(first, first, send_sem.at[32], fin_sem, at(0, e, 0))
        taken(here, finy_sem.at[d - 1])
        second = chunk(x, cy, cut, late - cut)
        for e in ALONG_Y:
            put(second, second, send_sem.at[32], fin_sem, at(e, 0, 0))

    taken(final.at[pl.ds(0, 18 * EARLY), :], early_sem)
    ahead = dot3(split(early[0]), left(w), NT) + dot3(split(early[1]), right(w), NT)
    for k in range(16):
        final[k * PART:k * PART + EARLY, :] = ahead[k * EARLY:(k + 1) * EARLY]

    ymat, zmat = lax.fori_loop(AHEAD, NS_ITERS - 2, refine, (ymat, zmat))
    ymat, zmat = split(ymat), split(zmat)
    middle = split(1.5 * eye - 0.5 * dot3(zmat, ymat, NN))
    scaled = split(dot3(middle, zmat, NN) * (jnp.sqrt(F32(GENES)) / jnp.sqrt(norm)))

    taken(final.at[pl.ds(0, 9 * late), :], fin_sem)
    hi, lo = split(final[...])
    fh[...] = hi
    fl[...] = lo
    shares = dot2(x_ref[...], (fh[...], fl[...]), NN)
    prod[...] = dot3(scaled, split(shares), NT).reshape(NZ, 2, 16, ELL)

    put(prod.at[:, 1 - c], prodcore, send_sem.at[33], pr_sem.at[0], sibling)
    sent(prodcore, send_sem.at[33])
    taken(prodcore, pr_sem.at[0])
    prodhalf[...] = prod[:, c] + prodcore[...]
    for i in ALONG_Z:
        k = lax.rem(z + i, NZ)
        put(prodhalf.at[k], prodrs.at[i - 1], send_sem.at[34], pr_sem.at[1], (cell, k * 2 + c))
    sent(prodrs, send_sem.at[34])
    basis_ref[...] = dot3(scaled, (fh[...], fl[...]), NT)
    store_basis = pltpu.make_async_copy(basis_ref, basis_hbm, load_sem.at[0])
    store_basis.start()
    taken(prodrs, pr_sem.at[1])
    scores = prodhalf[z]
    for i in range(NZ - 1):
        scores = scores + prodrs[i]
    squares = jnp.sum(scores * scores, axis=1, keepdims=True)
    lane = lax.broadcasted_iota(jnp.int32, (8, 128), 1)
    sq[cell] = jnp.where(
        lane < 64, jnp.broadcast_to(squares[:8], (8, 128)), jnp.broadcast_to(squares[8:], (8, 128))
    )
    for dx, dy in PLANES[3]:
        put(sq.at[cell], sq.at[cell], send_sem.at[35], sq_sem, at(dx, dy, 0))
    sent(sq.at[pl.ds(0, 15)], send_sem.at[35])
    taken(sq.at[pl.ds(0, 15)], sq_sem)
    squares = jnp.sum(sq[...], axis=0)
    spread = jnp.concatenate([squares[:, :1], squares[:, 64:65]], axis=0) * (1.0 / CELLS)
    scores_ref[...] = scores / jnp.sqrt(spread + 1e-05)
    store_basis.wait()
    for like, sem in sends:
        taken(like, sem)


def handed_on(basis_in, scores_in, basis_out, scores_out, held, held_scores, in_sem, out_sem):
    count = STRIPS
    strip = ELL // count
    first = pltpu.make_async_copy(scores_in, held_scores, in_sem.at[count])
    first.start()
    reads = []
    for i in range(count):
        spot = pl.ds(i * strip, strip)
        read = pltpu.make_async_copy(basis_in.at[spot, :], held.at[spot, :], in_sem.at[i])
        read.start()
        reads.append(read)
    first.wait()
    writes = [pltpu.make_async_copy(held_scores, scores_out, out_sem.at[count])]
    writes[0].start()
    for i in range(count):
        spot = pl.ds(i * strip, strip)
        reads[i].wait()
        write = pltpu.make_async_copy(held.at[spot, :], basis_out.at[spot, :], out_sem.at[i])
        write.start()
        writes.append(write)
    for write in writes:
        write.wait()


def on_device(expression, mixing):
    vmem = pl.BlockSpec(memory_space=pltpu.VMEM)
    dma = pltpu.SemaphoreType.DMA

    def buf(*shape, kind=F32):
        return pltpu.VMEM(shape, kind)

    basis, scores = pl.pallas_call(
        kernel,
        out_shape=(
            jax.ShapeDtypeStruct((ELL, LOCAL), F32),
            jax.ShapeDtypeStruct((16, ELL), F32),
        ),
        in_specs=[pl.BlockSpec(memory_space=pltpu.HBM)] * 2,
        out_specs=(pl.BlockSpec(memory_space=pltpu.HBM), vmem),
        scratch_shapes=[
            buf(ELL, LOCAL, kind=BF16), buf(4, ELL, 2 * ELL, kind=BF16), buf(ELL, LOCAL),
            buf(LOCAL, ELL), buf(NY, QUART, ELL), buf(5, 2, 256, 128), buf(5, 2, 128, 128),
            buf(5, 2, 128, 128), buf(NYZ - 1, 5, 8, 128), buf(2, 15, 2, 16, 128), buf(2, NZ, 2, 16, 128), buf(5, 2, 256, 128),
            buf(2, 256, 128), buf(2, 128, 128), buf(2, 128, 128), buf(NZ - 1, 2, 16, 128),
            buf(NY, 2, 256, 128),
            buf(QUART, ELL), buf(QUART, ELL), buf(2 * PART, ELL), buf(PART, ELL),
            buf(2, 2 * PART, ELL), buf(2, PART, ELL), buf(2, 2, 2, 256, 128), buf(2, 16 * EARLY, ELL), buf(LOCAL, ELL),
            buf(4, QUART, ELL, kind=BF16),
            buf(2, 2 * ELL, 2 * ELL, kind=BF16), buf(2, 2 * ELL, 2 * ELL, kind=BF16),
            buf(LOCAL, ELL, kind=BF16), buf(LOCAL, ELL, kind=BF16),
            buf(NZ, 2, 16, ELL), buf(NZ, 16, ELL), buf(NZ, 16, ELL), buf(NZ - 1, 16, ELL),
            buf(16, 8, 128),
            dma((2,)), dma((37,)), dma((4,)), dma((4,)), dma((4,)), dma((4,)), dma((2,)),
            dma, dma((5,)), dma((2,)), dma((4,)), dma((3,)), dma((3,)), dma, dma, dma((3,)), dma((3,)), dma((2,)), dma,
        ],
        compiler_params=pltpu.CompilerParams(
            collective_id=0, has_side_effects=True, vmem_limit_bytes=62 * 2**20
        ),
    )(expression, mixing)
    hbm = pl.BlockSpec(memory_space=pltpu.HBM)
    basis, scores = pl.pallas_call(
        handed_on,
        out_shape=(
            jax.ShapeDtypeStruct((ELL, LOCAL), F32),
            jax.ShapeDtypeStruct((16, ELL), F32),
        ),
        in_specs=[hbm, hbm],
        out_specs=(hbm, hbm),
        scratch_shapes=[buf(ELL, LOCAL), buf(16, ELL), dma((STRIPS + 1,)), dma((STRIPS + 1,))],
    )(basis, scores)
    return basis, scores.T


def solution(mesh):
    return jax.shard_map(
        on_device,
        mesh=mesh,
        in_specs=(P("cell", "gene"), P()),
        out_specs=(P(None, "gene"), P("cell", "gene")),
        check_vma=False,
    )
```

```python
import jax
import jax.numpy as jnp
from jax import lax
from jax.experimental import pallas as pl
from jax.experimental.pallas import tpu as pltpu
from jax.sharding import PartitionSpec as P

GENES = 20480
CELLS = 4096
ELL = 256
NS_ITERS = 8
AHEAD = 2
STRIPS = 4
NY, NX, NZ = 4, 4, 8
NYZ = NY * NZ
LOCAL = GENES // 16
QUART = LOCAL // NY
PART = LOCAL // 16
EARLY = PART * 7 // 10
MESH = pl.DeviceIdType.MESH
F32 = jnp.float32
BF16 = jnp.bfloat16
NT = (((1,), (1,)), ((), ()))
NN = (((1,), (0,)), ((), ()))
TN = (((0,), (0,)), ((), ()))


def hops(d, n):
    return min(d, n - d)


ALONG_Y = sorted(range(1, NY), key=lambda d: -hops(d, NY))
ALONG_Z = sorted(range(1, NZ), key=lambda d: -hops(d, NZ))
OTHERS = sorted(
    ((dy, dz) for dy in range(NY) for dz in range(NZ) if dy or dz),
    key=lambda d: -hops(d[0], NY) - hops(d[1], NZ),
)
PLANES = {
    2: sorted(
        ((dx, dy) for dx in range(2) for dy in range(NY) if dx or dy),
        key=lambda d: -d[0] - hops(d[1], NY),
    ),
    3: sorted(
        ((dx, dy) for dx in range(NX) for dy in range(NY) if dx or dy),
        key=lambda d: -hops(d[0], NX) - hops(d[1], NY),
    ),
}


def split(a):
    hi = a.astype(BF16)
    return hi, (a - hi.astype(F32)).astype(BF16)


def dot(a, b, dims):
    return lax.dot_general(a, b, dims, preferred_element_type=F32)


def dot2(a, b, dims):
    return dot(a, b[0], dims) + dot(a, b[1], dims)


def dot3(a, b, dims):
    return dot(a[0], b[0], dims) + (dot(a[0], b[1], dims) + dot(a[1], b[0], dims))


def joined(pair):
    return jnp.concatenate([pair[0], pair[1]], axis=1)


def halves(ref, block):
    ref[0] = block[:, :128]
    ref[1] = block[:, 128:]


def kernel(
    x_hbm, mix_hbm, basis_hbm, scores_ref,
    x_ref, mix_ref, basis_ref, xt, rx, part, corebuf, half, rsbuf, cellbuf, zbuf, total,
    selfp, selfcore, selfhalf, selfrs, selfall,
    low, high, quad, mid, pairbuf2, pairbuf3, pairself, early, final,
    stash, gh, gl, fh, fl, prod, prodcore, prodhalf, prodrs, sq,
    load_sem, send_sem, core_sem, rs_sem, ag_sem, cag_sem, z_sem,
    a2a_sem, self_sem, pair_sem, pself_sem, earlyx_sem, earlyy_sem, early_sem, fin_sem, finx_sem, finy_sem, pr_sem, sq_sem,
):
    cell, gene = lax.axis_index("cell"), lax.axis_index("gene")
    x, y = cell // NY, cell % NY
    z, c = gene // 2, gene % 2
    yz = y * NZ + z
    sends = []

    def put(src, dst, send, recv, to):
        copy = pltpu.make_async_remote_copy(
            src_ref=src, dst_ref=dst, send_sem=send, recv_sem=recv,
            device_id=to, device_id_type=MESH,
        )
        copy.start()
        return copy

    def taken(like, sem):
        pltpu.make_async_copy(like, like, sem).wait()

    def sent(like, sem):
        sends.append((like, sem))

    def at(dx, dy, dz):
        return (lax.rem(x + dx, NX) * NY + lax.rem(y + dy, NY), lax.rem(z + dz, NZ) * 2 + c)

    def paired(dx, dy):
        return ((x + dx * (1 - 2 * (x % 2))) * NY + lax.rem(y + dy, NY), gene)

    load_x = pltpu.make_async_copy(x_hbm, x_ref, load_sem.at[0])
    load_mix = pltpu.make_async_copy(mix_hbm, mix_ref, load_sem.at[1])
    load_x.start()
    load_mix.start()
    sibling = (cell, z * 2 + (1 - c))

    barrier = pltpu.get_barrier_semaphore()

    def greet(to):
        pl.semaphore_signal(barrier, inc=1, device_id=to, device_id_type=MESH)

    for d in ALONG_Z[:3]:
        greet(at(0, 0, d))
    for d in ALONG_Y:
        greet(at(0, d, 0))
    for d in ALONG_Z[3:]:
        greet(at(0, 0, d))
    for d in ALONG_Y:
        greet(at(d, 0, 0))
    greet(sibling)
    load_x.wait()

    for t in range(LOCAL // 128):
        xt[t * 128:(t + 1) * 128, :] = x_ref[:, t * 128:(t + 1) * 128].astype(F32).T
    own = pl.ds(pl.multiple_of(y * QUART, QUART), QUART)
    rx[y] = xt[own, :]
    xb = x_ref[...]
    halves(selfp, dot(xb, xb, NT))
    pl.semaphore_wait(barrier, NZ - 1 + NY - 1 + NX - 1 + 1)

    for i in ALONG_Y:
        q = lax.rem(y + i, NY)
        put(
            xt.at[pl.ds(pl.multiple_of(q * QUART, QUART), QUART), :], rx.at[y],
            send_sem.at[0], a2a_sem, (x * NY + q, gene),
        )
    sent(xt.at[pl.ds(0, 3 * QUART), :], send_sem.at[0])

    def rows(base, count):
        return pl.ds(pl.multiple_of(base, count), count)

    mine = rows(c * 128, 128)
    theirs = rows((1 - c) * 128, 128)

    put(selfp.at[:, theirs, :], selfcore, send_sem.at[1], self_sem.at[0], sibling)
    sent(selfcore, send_sem.at[1])
    taken(selfcore, self_sem.at[0])
    selfhalf[...] = selfp[:, mine, :] + selfcore[...]
    for i in ALONG_Z:
        k = lax.rem(z + i, NZ)
        put(
            selfhalf.at[:, rows(k * 16, 16), :], selfrs.at[i - 1],
            send_sem.at[2], self_sem.at[1], (cell, k * 2 + c),
        )
    sent(selfrs, send_sem.at[2])
    taken(selfrs, self_sem.at[1])
    piece = selfhalf[:, rows(z * 16, 16), :]
    for i in range(NZ - 1):
        piece = piece + selfrs[i]
    place = rows(c * 128 + z * 16, 16)
    selfall[y, :, place, :] = piece
    for i in ALONG_Z:
        k = lax.rem(z + i, NZ)
        put(
            selfall.at[y, :, place, :], selfall.at[y, :, place, :],
            send_sem.at[3], self_sem.at[2], (cell, k * 2 + c),
        )
    sent(selfrs, send_sem.at[3])
    taken(selfrs, self_sem.at[2])
    for i in ALONG_Y:
        q = lax.rem(y + i, NY)
        put(
            selfall.at[y, :, mine, :], selfall.at[y, :, mine, :],
            send_sem.at[4], self_sem.at[3], (x * NY + q, gene),
        )
    sent(selfall.at[pl.ds(0, 3), :, pl.ds(0, 128), :], send_sem.at[4])

    taken(rx.at[pl.ds(0, 3)], a2a_sem)

    def reduced(level, at_block, count, cross, scattering=None, summing=None, gathering=None):
        block = pl.ds(at_block, count)
        sem = 5 + 5 * level
        cross(1 - c)
        put(
            part.at[block, :, theirs, :], corebuf.at[block],
            send_sem.at[sem], core_sem.at[level], sibling,
        )
        sent(corebuf.at[block], send_sem.at[sem])
        cross(c)
        taken(corebuf.at[block], core_sem.at[level])
        half[block] = part[block, :, mine, :] + corebuf[block]
        if level < 2:
            for dy, dz in OTHERS:
                k = lax.rem(y + dy, NY) * NZ + lax.rem(z + dz, NZ)
                put(
                    half.at[block, k // 16, rows((k % 16) * 8, 8), :],
                    rsbuf.at[dy * NZ + dz - 1, block],
                    send_sem.at[sem + 1], rs_sem.at[level], at(0, dy, dz),
                )
            sent(rsbuf.at[:, block], send_sem.at[sem + 1])
            if scattering is not None:
                scattering()
            taken(rsbuf.at[:, block], rs_sem.at[level])
            tile = half[block, yz // 16, rows((yz % 16) * 8, 8), :]
            for i in range(NYZ - 1):
                tile = tile + rsbuf[i, block]
            piece = total.at[block, yz // 16, rows(c * 128 + (yz % 16) * 8, 8), :]
            piece[...] = tile
            for dy, dz in OTHERS:
                put(piece, piece, send_sem.at[sem + 3], ag_sem.at[level], at(0, dy, dz))
            sent(rsbuf.at[:, block], send_sem.at[sem + 3])
            if gathering is not None:
                gathering()
            taken(rsbuf.at[:, block], ag_sem.at[level])
        else:
            slot = level - 2
            peers = PLANES[level]
            strip = 128 // (len(peers) + 1)
            inbox = cellbuf.at[slot, pl.ds(0, len(peers)), :, pl.ds(0, strip), :]
            whose = (lambda dx, dy: paired(dx, dy)) if level == 2 else (lambda dx, dy: at(dx, dy, 0))
            index = (lambda to: to % 8) if level == 2 else (lambda to: to)
            own = half[at_block, :, rows(index(cell) * strip, strip), :]
            for dx, dy in peers:
                to = whose(dx, dy)
                put(
                    half.at[at_block, :, rows(index(to[0]) * strip, strip), :],
                    cellbuf.at[slot, dx * NY + dy - 1, :, pl.ds(0, strip), :],
                    send_sem.at[sem + 1], rs_sem.at[level], to,
                )
            sent(inbox, send_sem.at[sem + 1])
            taken(inbox, rs_sem.at[level])
            for i in range(len(peers)):
                own = own + cellbuf[slot, i, :, :strip, :]
            share = zbuf.at[slot, z, :, pl.ds(0, strip), :]
            share[...] = own
            for dz in ALONG_Z:
                put(share, share, send_sem.at[sem + 2], z_sem.at[slot], at(0, 0, dz))
            inbox = zbuf.at[slot, pl.ds(0, NZ - 1), :, pl.ds(0, strip), :]
            sent(inbox, send_sem.at[sem + 2])
            if summing is not None:
                summing()
            taken(inbox, z_sem.at[slot])
            own = zbuf[slot, 0, :, :strip, :]
            for i in range(1, NZ):
                own = own + zbuf[slot, i, :, :strip, :]
            piece = total.at[at_block, :, rows(c * 128 + index(cell) * strip, strip), :]
            piece[...] = own
            for dx, dy in peers:
                put(piece, piece, send_sem.at[sem + 3], ag_sem.at[level], whose(dx, dy))
            inbox = cellbuf.at[slot, pl.ds(0, len(peers)), :, pl.ds(0, strip), :]
            sent(inbox, send_sem.at[sem + 3])
            gathering()
            taken(inbox, ag_sem.at[level])
        put(
            total.at[block, :, mine, :], total.at[block, :, mine, :],
            send_sem.at[sem + 4], cag_sem.at[level], sibling,
        )
        sent(corebuf.at[block], send_sem.at[sem + 4])
        taken(corebuf.at[block], cag_sem.at[level])

    def prepare(level, lower, upper, slot=0):
        for at_row, gram in ((0, lower), (ELL, upper)):
            spot = slice(at_row, at_row + ELL)
            gh[slot, spot, spot], gl[slot, spot, spot] = split(gram)
        mix = mix_ref[level]
        first = dot2(mix[:, :ELL], (gh[slot, :ELL, :ELL], gl[slot, :ELL, :ELL]), NN)
        second = dot2(mix[:, ELL:], (gh[slot, ELL:, ELL:], gl[slot, ELL:, ELL:]), NN)
        squares = jnp.sum(lower * lower, keepdims=True) + jnp.sum(upper * upper, keepdims=True)
        return first, second, squares

    def weights(level, cross, ready, slot=0):
        first, second, squares = ready
        inv = 1.0 / jnp.sqrt(squares + 2.0 * jnp.sum(cross * cross, keepdims=True) + 1e-06)
        over, under = split(cross), split(cross.T)
        gh[slot, :ELL, ELL:], gl[slot, :ELL, ELL:] = over
        gh[slot, ELL:, :ELL], gl[slot, ELL:, :ELL] = under
        mix = mix_ref[level]
        once = jnp.concatenate(
            [first + dot2(mix[:, ELL:], under, NN), second + dot2(mix[:, :ELL], over, NN)], axis=1
        )
        twice = dot3(split(once), (gh[slot], gl[slot]), NN)
        return 0.5 * mix.astype(F32) + once * inv - (0.5 * twice) * (inv * inv)

    def own_gram(w, slot=0):
        return dot3(split(dot3(w, (gh[slot], gl[slot]), NN)), w, NT)

    def left(w):
        return w[0][:, :ELL], w[1][:, :ELL]

    def right(w):
        return w[0][:, ELL:], w[1][:, ELL:]

    def stashed(base, count):
        at_rows = rows(base, count) if base is not None else pl.ds(0, count)
        return (stash[0, at_rows, :], stash[1, at_rows, :]), (stash[2, at_rows, :], stash[3, at_rows, :])

    def sketched(w, base, count):
        lower, upper = stashed(base, count)
        return dot3(lower, left(w), NT) + dot3(upper, right(w), NT)

    def crossed(at_block, count):
        def cross(side):
            side_rows = rows(side * 128, 128)
            lower = stash[0, :count, side_rows], stash[1, :count, side_rows]
            block = dot3(lower, stashed(None, count)[1], TN)
            part[at_block, 0, side_rows, :] = block[:, :128]
            part[at_block, 1, side_rows, :] = block[:, 128:]

        return cross

    def keep(lower, upper):
        count = lower.shape[0]
        stash[0, :count], stash[1, :count] = split(lower)
        stash[2, :count], stash[3, :count] = split(upper)

    for i in range(NY):
        stash[i] = rx[i].astype(BF16)

    def cross_batches(side):
        side_rows = rows(side * 128, 128)
        for p in range(2):
            block = dot(stash[2 * p, :, side_rows], stash[2 * p + 1], TN)
            part[p, 0, side_rows, :] = block[:, :128]
            part[p, 1, side_rows, :] = block[:, 128:]

    ready = []

    def swap_selves():
        taken(selfall.at[pl.ds(0, 3), :, pl.ds(0, 128), :], self_sem.at[3])
        put(
            selfall.at[:, :, mine, :], selfall.at[:, :, mine, :],
            send_sem.at[25], self_sem.at[4], sibling,
        )
        sent(selfall.at[:, :, pl.ds(0, 128), :], send_sem.at[25])
        load_mix.wait()
        taken(selfall.at[:, :, pl.ds(0, 128), :], self_sem.at[4])
        for p in range(2):
            ready.append(prepare(0, joined(selfall[2 * p]), joined(selfall[2 * p + 1]), p))

    reduced(0, 0, 2, cross_batches, gathering=swap_selves)
    kept = []
    for p, sketch in ((0, low), (1, high)):
        w = split(weights(0, joined(total[p]), ready[p], p))
        sketch[...] = dot2(stash[2 * p], left(w), NT) + dot2(stash[2 * p + 1], right(w), NT)
        kept.append(w)

    keep(low[...], high[...])
    grams = []
    reduced(
        1, 2, 1, crossed(2, QUART),
        scattering=lambda: grams.extend(own_gram(kept[p], p) for p in range(2)),
        gathering=lambda: ready.append(prepare(1, *grams)),
    )
    w = split(weights(1, joined(total[2]), ready[-1]))

    def order(cx, cy):
        return cy * 4 + cx % 2 * 2 + cx // 2

    for level, step, src, buf in ((2, 1, quad, pairbuf2), (3, 2, mid, pairbuf3)):
        slot = level - 2
        bit = x // step % 2
        to = ((x + step * (1 - 2 * bit)) * NY + y, gene)
        count = buf.shape[1]
        src[...] = sketched(w, (1 - bit) * count, count)
        put(src, buf.at[bit], send_sem.at[26 + slot], pair_sem.at[slot], to)
        sent(buf.at[0], send_sem.at[26 + slot])
        buf[bit] = sketched(w, bit * count, count)
        halves(pairself.at[slot, bit], own_gram(w))
        share = pairself.at[slot, bit, :, mine, :]
        put(share, share, send_sem.at[28 + slot], pself_sem.at[slot], to)
        sent(pairself.at[slot, 0, :, pl.ds(0, 128), :], send_sem.at[28 + slot])

        def summing():
            here = early.at[:, rows(order(x, y) * EARLY, EARLY), :]
            here[...] = buf[:, :EARLY, :]
            for d in ALONG_Y:
                put(here, here, send_sem.at[36], earlyx_sem.at[d - 1], at(d, 0, 0))
                put(here, here, send_sem.at[36], earlyy_sem.at[d - 1], at(0, d, 0))
            sent(early.at[:, pl.ds(0, 15 * EARLY), :], send_sem.at[36])

        def gathering():
            taken(pairself.at[slot, 0, :, pl.ds(0, 128), :], pself_sem.at[slot])
            across = pairself.at[slot, 1 - bit, :, mine, :]
            put(across, across, send_sem.at[30 + slot], pself_sem.at[2 + slot], sibling)
            sent(pairself.at[slot, 0, :, pl.ds(0, 128), :], send_sem.at[30 + slot])
            if level == 3:
                for d in (1, 3, 2):
                    cx, cy = lax.rem(x + NX - d, NX), lax.rem(y + NY - d, NY)
                    taken(early.at[:, pl.ds(0, EARLY), :], earlyx_sem.at[d - 1])
                    first = early.at[0, rows(order(cx, y) * EARLY, EARLY), :]
                    for e in ALONG_Y:
                        put(first, first, send_sem.at[36], early_sem, at(0, e, 0))
                    taken(early.at[:, pl.ds(0, EARLY), :], earlyy_sem.at[d - 1])
                    second = early.at[1, rows(order(x, cy) * EARLY, EARLY), :]
                    for e in ALONG_Y:
                        put(second, second, send_sem.at[36], early_sem, at(e, 0, 0))
            taken(pairself.at[slot, 0, :, pl.ds(0, 128), :], pself_sem.at[2 + slot])
            ready.append(prepare(level, joined(pairself[slot, 0]), joined(pairself[slot, 1])))

        taken(buf.at[0], pair_sem.at[slot])
        keep(buf[0], buf[1])
        reduced(
            level, level + 1, 1, crossed(level + 1, count),
            summing=summing if level == 3 else None, gathering=gathering,
        )
        w = split(weights(level, joined(total[level + 1]), ready[-1]))

    def chunk(cx, cy, skip, count):
        return final.at[pl.ds(pl.multiple_of(order(cx, cy) * PART + EARLY + skip, 8), count), :]

    late = PART - EARLY
    cut = (late // 8 + 1) // 2 * 8
    here = chunk(x, y, 0, late)
    here[...] = sketched(w, None, PART)[EARLY:]
    for d in ALONG_Y:
        put(here, here, send_sem.at[32], finx_sem.at[d - 1], at(d, 0, 0))
        put(here, here, send_sem.at[32], finy_sem.at[d - 1], at(0, d, 0))
    sent(final.at[pl.ds(0, 15 * late), :], send_sem.at[32])

    gram = own_gram(w)
    norm = jnp.sqrt(jnp.sum(gram * gram, keepdims=True) + 1e-06)
    eye = (
        lax.broadcasted_iota(jnp.int32, (ELL, ELL), 0) == lax.broadcasted_iota(jnp.int32, (ELL, ELL), 1)
    ).astype(F32)
    ymat = gram * (1.0 / norm)
    middle = 1.5 * eye - 0.5 * ymat
    zmat = middle
    ymat = dot3(split(ymat), split(middle), NN)

    def refine(step, carry):
        ymat, zmat = split(carry[0]), split(carry[1])
        middle = split(1.5 * eye - 0.5 * dot3(zmat, ymat, NN))
        return dot3(ymat, middle, NN), dot3(middle, zmat, NN)

    ymat, zmat = lax.fori_loop(0, AHEAD, refine, (ymat, zmat))

    for d in (1, 3, 2):
        cx, cy = lax.rem(x + NX - d, NX), lax.rem(y + NY - d, NY)
        taken(here, finx_sem.at[d - 1])
        first = chunk(cx, y, 0, cut)
        for e in ALONG_Y:
            put(first, first, send_sem.at[32], fin_sem, at(0, e, 0))
        taken(here, finy_sem.at[d - 1])
        second = chunk(x, cy, cut, late - cut)
        for e in ALONG_Y:
            put(second, second, send_sem.at[32], fin_sem, at(e, 0, 0))

    taken(final.at[pl.ds(0, 18 * EARLY), :], early_sem)
    ahead = dot3(split(early[0]), left(w), NT) + dot3(split(early[1]), right(w), NT)
    for k in range(16):
        final[k * PART:k * PART + EARLY, :] = ahead[k * EARLY:(k + 1) * EARLY]

    ymat, zmat = lax.fori_loop(AHEAD, NS_ITERS - 2, refine, (ymat, zmat))
    ymat, zmat = split(ymat), split(zmat)
    middle = split(1.5 * eye - 0.5 * dot3(zmat, ymat, NN))
    scaled = split(dot3(middle, zmat, NN) * (jnp.sqrt(F32(GENES)) / jnp.sqrt(norm)))

    taken(final.at[pl.ds(0, 9 * late), :], fin_sem)
    hi, lo = split(final[...])
    fh[...] = hi
    fl[...] = lo
    shares = dot2(x_ref[...], (fh[...], fl[...]), NN)
    prod[...] = dot3(scaled, split(shares), NT).reshape(NZ, 2, 16, ELL)

    put(prod.at[:, 1 - c], prodcore, send_sem.at[33], pr_sem.at[0], sibling)
    sent(prodcore, send_sem.at[33])
    taken(prodcore, pr_sem.at[0])
    prodhalf[...] = prod[:, c] + prodcore[...]
    for i in ALONG_Z:
        k = lax.rem(z + i, NZ)
        put(prodhalf.at[k], prodrs.at[i - 1], send_sem.at[34], pr_sem.at[1], (cell, k * 2 + c))
    sent(prodrs, send_sem.at[34])
    basis_ref[...] = dot3(scaled, (fh[...], fl[...]), NT)
    store_basis = pltpu.make_async_copy(basis_ref, basis_hbm, load_sem.at[0])
    store_basis.start()
    taken(prodrs, pr_sem.at[1])
    scores = prodhalf[z]
    for i in range(NZ - 1):
        scores = scores + prodrs[i]
    squares = jnp.sum(scores * scores, axis=1, keepdims=True)
    lane = lax.broadcasted_iota(jnp.int32, (8, 128), 1)
    sq[cell] = jnp.where(
        lane < 64, jnp.broadcast_to(squares[:8], (8, 128)), jnp.broadcast_to(squares[8:], (8, 128))
    )
    for dx, dy in PLANES[3]:
        put(sq.at[cell], sq.at[cell], send_sem.at[35], sq_sem, at(dx, dy, 0))
    sent(sq.at[pl.ds(0, 15)], send_sem.at[35])
    taken(sq.at[pl.ds(0, 15)], sq_sem)
    squares = jnp.sum(sq[...], axis=0)
    spread = jnp.concatenate([squares[:, :1], squares[:, 64:65]], axis=0) * (1.0 / CELLS)
    scores_ref[...] = scores / jnp.sqrt(spread + 1e-05)
    store_basis.wait()
    for like, sem in sends:
        taken(like, sem)


def handed_on(basis_in, scores_in, basis_out, scores_out, held, held_scores, in_sem, out_sem):
    count = STRIPS
    strip = ELL // count
    first = pltpu.make_async_copy(scores_in, held_scores, in_sem.at[count])
    first.start()
    reads = []
    for i in range(count):
        spot = pl.ds(i * strip, strip)
        read = pltpu.make_async_copy(basis_in.at[spot, :], held.at[spot, :], in_sem.at[i])
        read.start()
        reads.append(read)
    first.wait()
    writes = [pltpu.make_async_copy(held_scores, scores_out, out_sem.at[count])]
    writes[0].start()
    for i in range(count):
        spot = pl.ds(i * strip, strip)
        reads[i].wait()
        write = pltpu.make_async_copy(held.at[spot, :], basis_out.at[spot, :], out_sem.at[i])
        write.start()
        writes.append(write)
    for write in writes:
        write.wait()


def on_device(expression, mixing):
    vmem = pl.BlockSpec(memory_space=pltpu.VMEM)
    dma = pltpu.SemaphoreType.DMA

    def buf(*shape, kind=F32):
        return pltpu.VMEM(shape, kind)

    basis, scores = pl.pallas_call(
        kernel,
        out_shape=(
            jax.ShapeDtypeStruct((ELL, LOCAL), F32),
            jax.ShapeDtypeStruct((16, ELL), F32),
        ),
        in_specs=[pl.BlockSpec(memory_space=pltpu.HBM)] * 2,
        out_specs=(pl.BlockSpec(memory_space=pltpu.HBM), vmem),
        scratch_shapes=[
            buf(ELL, LOCAL, kind=BF16), buf(4, ELL, 2 * ELL, kind=BF16), buf(ELL, LOCAL),
            buf(LOCAL, ELL), buf(NY, QUART, ELL), buf(5, 2, 256, 128), buf(5, 2, 128, 128),
            buf(5, 2, 128, 128), buf(NYZ - 1, 5, 8, 128), buf(2, 15, 2, 16, 128), buf(2, NZ, 2, 16, 128), buf(5, 2, 256, 128),
            buf(2, 256, 128), buf(2, 128, 128), buf(2, 128, 128), buf(NZ - 1, 2, 16, 128),
            buf(NY, 2, 256, 128),
            buf(QUART, ELL), buf(QUART, ELL), buf(2 * PART, ELL), buf(PART, ELL),
            buf(2, 2 * PART, ELL), buf(2, PART, ELL), buf(2, 2, 2, 256, 128), buf(2, 16 * EARLY, ELL), buf(LOCAL, ELL),
            buf(4, QUART, ELL, kind=BF16),
            buf(2, 2 * ELL, 2 * ELL, kind=BF16), buf(2, 2 * ELL, 2 * ELL, kind=BF16),
            buf(LOCAL, ELL, kind=BF16), buf(LOCAL, ELL, kind=BF16),
            buf(NZ, 2, 16, ELL), buf(NZ, 16, ELL), buf(NZ, 16, ELL), buf(NZ - 1, 16, ELL),
            buf(16, 8, 128),
            dma((2,)), dma((37,)), dma((4,)), dma((4,)), dma((4,)), dma((4,)), dma((2,)),
            dma, dma((5,)), dma((2,)), dma((4,)), dma((3,)), dma((3,)), dma, dma, dma((3,)), dma((3,)), dma((2,)), dma,
        ],
        compiler_params=pltpu.CompilerParams(
            collective_id=0, has_side_effects=True, vmem_limit_bytes=62 * 2**20
        ),
    )(expression, mixing)
    hbm = pl.BlockSpec(memory_space=pltpu.HBM)
    basis, scores = pl.pallas_call(
        handed_on,
        out_shape=(
            jax.ShapeDtypeStruct((ELL, LOCAL), F32),
            jax.ShapeDtypeStruct((16, ELL), F32),
        ),
        in_specs=[hbm, hbm],
        out_specs=(hbm, hbm),
        scratch_shapes=[buf(ELL, LOCAL), buf(16, ELL), dma((STRIPS + 1,)), dma((STRIPS + 1,))],
    )(basis, scores)
    return basis, scores.T


def solution(mesh):
    return jax.shard_map(
        on_device,
        mesh=mesh,
        in_specs=(P("cell", "gene"), P()),
        out_specs=(P(None, "gene"), P("cell", "gene")),
        check_vma=False,
    )
```
